128 devices in a mesh: seq: 16 (over x, z_hi, core), win: 8 (over y, z_lo).
Axes of the slice: x: 4, y: 4, z: 4 (z_hi: 2, z_lo: 2; z = z_hi * 2 + z_lo), core: 2. Of those that a mesh axis runs over, the one named last changes fastest.
Arguments:
- tokens: bfloat16 [16, 2048, 512], P('win', 'seq'), may hold values from -6 to 6
- lengths: int32 [16], P('win'), may hold values from 1536 to 2048, as said below
- gain_one: float32 [512], replicated, may hold values from 0.1 to 1.9
- bias_one: float32 [512], replicated, may hold values from -3 to 3
- weight_query: bfloat16 [512, 512], replicated, may hold values from -0.25 to 0.25
- weight_key: bfloat16 [512, 512], replicated, may hold values from -0.25 to 0.25
- weight_value: bfloat16 [512, 512], replicated, may hold values from -0.25 to 0.25
- weight_out: bfloat16 [512, 512], replicated, may hold values from -2 to 2
- gain_two: float32 [512], replicated, may hold values from 0.1 to 1.9
- bias_two: float32 [512], replicated, may hold values from -3 to 3
- weight_gate: bfloat16 [512, 2048], replicated, may hold values from -0.25 to 0.25
- weight_up: bfloat16 [512, 2048], replicated, may hold values from -0.25 to 0.25
- weight_down: bfloat16 [2048, 512], replicated, may hold values from -0.25 to 0.25
- cotangent: bfloat16 [16, 2048, 512], P('win', 'seq'), may hold values from -6 to 6
Outputs:
- output: float32 [16, 2048, 512], P('win', 'seq')
- grad_tokens: float32 [16, 2048, 512], P('win', 'seq')
- grad_gain_one: float32 [512], replicated
- grad_bias_one: float32 [512], replicated
- grad_query: float32 [512, 512], replicated
- grad_key: float32 [512, 512], replicated
- grad_value: float32 [512, 512], replicated
- grad_out: float32 [512, 512], replicated
- grad_gain_two: float32 [512], replicated
- grad_bias_two: float32 [512], replicated
- grad_gate: float32 [512, 2048], replicated
- grad_up: float32 [512, 2048], replicated
- grad_down: float32 [2048, 512], replicated
The draws below stay inside these ranges and needn't reach their ends.
Inputs may be any that keep to these rules, and one draw needn't show every extreme that they name: `lengths`: of the 2 consecutive windows that share an index of win, one, drawn from the seed, is longer than 1920; at least one window of all, drawn from the seed, has length 2048.
All inputs are finite; a program needn't handle non-finite values.
Results may differ from the reference program's by a relative error of at most 0.017.
Values may be sent and summed in bfloat16 or wider, within the bound.
No kernel may reach another device: no remote copies, remote signals or barrier semaphores. Data moves between devices by JAX's collectives and lax.ppermute only.
A program may use at most 192 MiB of HBM per device.

```python
import jax
import jax.numpy as jnp
from jax import lax

D = 512
HEADS = 16
HEAD_DIM = 32
FF = 2048
WIN_DEV = 2
LENGTH = 2048
SEQ_DEV = 128
WINDOWS = 16


def draw_lengths(key, part):
    key = jax.random.fold_in(key, 7)
    pick_key, length_key, long_key, group_key = jax.random.split(key, 4)
    groups = WINDOWS // WIN_DEV
    drawn = jax.random.randint(length_key, (WINDOWS,), 3 * LENGTH // 4, LENGTH + 1)
    spanning = jax.random.randint(long_key, (WINDOWS,), LENGTH - SEQ_DEV + 1, LENGTH + 1)
    chosen = jax.random.randint(pick_key, (groups, 1), 0, WIN_DEV)
    slots = jnp.arange(WIN_DEV, dtype=jnp.int32)[None, :]
    picked = slots == chosen
    full_group = jax.random.randint(group_key, (), 0, groups)
    group_ids = jnp.arange(groups, dtype=jnp.int32)[:, None]
    full = (picked & (group_ids == full_group)).reshape(WINDOWS)
    picked = picked.reshape(WINDOWS)
    result = jnp.where(picked, spanning, drawn)
    result = jnp.where(full, LENGTH, result)
    return result.astype(jnp.int32)


def block_scale(rng, dims, pieces, smallest, largest):
    factor_of, own = 1.0, jax.random.fold_in(rng, 6)
    for dim, shards_of in pieces:
        steps = jnp.exp(jax.random.uniform(jax.random.fold_in(own, dim), (shards_of,), jnp.float32, smallest / len(pieces), largest / len(pieces)))
        factor_of = factor_of * jnp.repeat(steps, dims[dim] // shards_of).reshape([-1 if axis == dim else 1 for axis in range(len(dims))])
    return factor_of


def scatter_about(key, extent, scale, limit, cuts=(), kind=jnp.bfloat16):
    values = scale * jax.random.normal(key, extent, jnp.float32)
    if cuts:
        values = values * block_scale(key, extent, cuts, -0.22, 0.18)
    return jnp.clip(values, -limit, limit).astype(kind)


def setup_inputs(seed: int = 0) -> dict:
    key_of = jax.random.split(jax.random.key(seed), 15)
    tokens = scatter_about(key_of[0], (WINDOWS, LENGTH, D), 1.0, 6.0, ((0, 8), (1, 16)))
    lengths = draw_lengths(jax.random.fold_in(key_of[14], 71), 0)
    gain_one = jnp.clip(1.0 + 0.18 * jax.random.normal(key_of[2], (D,), jnp.float32), 0.1, 1.9)
    bias_one = scatter_about(key_of[3], (D,), 0.5, 3.0, (), jnp.float32)
    weight_query = scatter_about(key_of[4], (D, D), D ** -0.5, 0.25)
    weight_key = scatter_about(key_of[5], (D, D), D ** -0.5, 0.25)
    weight_value = scatter_about(key_of[6], (D, D), D ** -0.5, 0.25)
    weight_out = scatter_about(key_of[7], (D, D), (D // 64) ** -0.5, 2.0)
    gain_two = jnp.clip(1.0 + 0.18 * jax.random.normal(key_of[8], (D,), jnp.float32), 0.1, 1.9)
    bias_two = scatter_about(key_of[9], (D,), 0.5, 3.0, (), jnp.float32)
    weight_gate = scatter_about(key_of[10], (D, FF), D ** -0.5, 0.25)
    weight_up = scatter_about(key_of[11], (D, FF), D ** -0.5, 0.25)
    weight_down = scatter_about(key_of[12], (FF, D), (FF // 4) ** -0.5, 0.25)
    cotangent = scatter_about(key_of[13], (WINDOWS, LENGTH, D), 1.0, 6.0, ((0, 8), (1, 16)))
    return dict(tokens=tokens, lengths=lengths, gain_one=gain_one, bias_one=bias_one, weight_query=weight_query, weight_key=weight_key, weight_value=weight_value, weight_out=weight_out, gain_two=gain_two, bias_two=bias_two, weight_gate=weight_gate, weight_up=weight_up, weight_down=weight_down, cotangent=cotangent)


epsilon = 1e-05
masked_score = -1e+30
highest = lax.Precision.HIGHEST

@jax.custom_vjp
def low(v):
    return lax.optimization_barrier(v.astype(jnp.bfloat16)).astype(jnp.float32)

@jax.custom_vjp
def low_back(v):
    return v

def low_keep(v):
    return (low(v), None)

def low_pass(kept, grad):
    return (grad,)

def back_keep(v):
    return (v, None)

def back_low(kept, grad):
    return (low(grad),)
low.defvjp(low_keep, low_pass)
low_back.defvjp(back_keep, back_low)

def matmul(left, right):
    return jnp.dot(left, right, precision=highest, preferred_element_type=jnp.float32)

def layer_norm(values, gain, shift):
    center = values - lax.optimization_barrier(jnp.mean(values, -1, keepdims=True))
    spread = lax.optimization_barrier(jnp.mean(center * center, -1, keepdims=True))
    return center * lax.rsqrt(spread + epsilon) * gain + shift

def rotary(values, positions, direction):
    halves = values.reshape(values.shape[:-1] + (HEADS, 2, HEAD_DIM // 2))
    inverse = 10000.0 ** (-jnp.arange(HEAD_DIM // 2, dtype=jnp.float32) * (2.0 / HEAD_DIM))
    angles = positions.astype(jnp.float32)[:, None] * inverse[None, :]
    cosine = jnp.cos(angles)[:, None, :]
    sine = direction * jnp.sin(angles)[:, None, :]
    first = halves[..., 0, :]
    second = halves[..., 1, :]
    turned = jnp.stack([first * cosine - second * sine, second * cosine + first * sine], -2)
    return turned.reshape(values.shape)

def window_forward(window_rows, length, params):
    gain_one, bias_one, weight_query, weight_key, weight_value, weight_out, gain_two, bias_two, weight_gate, weight_up, weight_down = params
    positions = jnp.arange(LENGTH, dtype=jnp.int32)
    normed = low(layer_norm(window_rows, gain_one, bias_one))
    queries = low(rotary(low_back(matmul(normed, weight_query)), positions, 1.0))
    keys_all = low(rotary(low_back(matmul(normed, weight_key)), positions, 1.0)).reshape(LENGTH, HEADS, HEAD_DIM)
    values_all = low(low_back(matmul(normed, weight_value))).reshape(LENGTH, HEADS, HEAD_DIM)
    usable = (positions < length)[None, None, :]
    rows_block = min(512, LENGTH)

    def attend(query_block):
        scores = jnp.einsum('qhd,khd->qhk', query_block, keys_all, precision=highest) * HEAD_DIM ** (-0.5)
        scores = jnp.where(usable, low_back(scores), masked_score)
        peak = lax.optimization_barrier(jnp.max(scores, -1, keepdims=True))
        weight = jnp.exp(scores - peak)
        probs = low(weight / lax.optimization_barrier(jnp.sum(weight, -1, keepdims=True)))
        return jnp.einsum('qhk,khd->qhd', probs, values_all, precision=highest)
    mixed = lax.map(jax.checkpoint(attend), queries.reshape(LENGTH // rows_block, rows_block, HEADS, HEAD_DIM))
    mixed = low(low_back(mixed.reshape(LENGTH, HEADS * HEAD_DIM)))
    residual = window_rows + low_back(matmul(mixed, weight_out))
    normed_two = low(layer_norm(residual, gain_two, bias_two))
    gate_pre = low_back(matmul(normed_two, weight_gate))
    up_pre = low_back(matmul(normed_two, weight_up))
    hidden = low(gate_pre * jax.nn.sigmoid(gate_pre) * up_pre)
    return residual + matmul(hidden, weight_down)

def reference(tokens, lengths, gain_one, bias_one, weight_query, weight_key, weight_value, weight_out, gain_two, bias_two, weight_gate, weight_up, weight_down, cotangent):
    inputs = tokens.astype(jnp.float32)
    params = (gain_one.astype(jnp.float32), bias_one.astype(jnp.float32), weight_query.astype(jnp.float32), weight_key.astype(jnp.float32), weight_value.astype(jnp.float32), weight_out.astype(jnp.float32), gain_two.astype(jnp.float32), bias_two.astype(jnp.float32), weight_gate.astype(jnp.float32), weight_up.astype(jnp.float32), weight_down.astype(jnp.float32))

    def whole_forward(inputs, params):

        def advance(carry, item):
            return (carry, jax.checkpoint(window_forward)(item[0], item[1], params))
        unused, outputs = lax.scan(advance, jnp.float32(0.0), (inputs, lengths))
        return outputs
    outputs, pullback = jax.vjp(whole_forward, inputs, params)
    grad_inputs, grads = pullback(cotangent.astype(jnp.float32))
    return (outputs, grad_inputs, grads[0], grads[1], grads[2], grads[3], grads[4], grads[5], grads[6], grads[7], grads[8], grads[9], grads[10])
```

```python
import functools
import math

import jax
import jax.numpy as jnp
import numpy as np
from jax import lax
from jax.experimental import pallas as pl
from jax.experimental.pallas import tpu as pltpu
from jax.sharding import Mesh
from jax.sharding import PartitionSpec as P

HEADS = 16
HEAD_DIM = 32
HALF = HEAD_DIM // 2
PARTS = 3 * HEAD_DIM
LENGTH = 2048
epsilon = 1e-05
masked_score = -1e30
BF = jnp.bfloat16
F32 = jnp.float32
inv_root = HEAD_DIM ** (-0.5)
score_scale = inv_root * math.log2(math.e)
VMEM_LIMIT = 60 * 1024 * 1024


def mm(a, b):
    return jnp.dot(a, b, preferred_element_type=F32)


def mm_nt(a, b):
    return lax.dot_general(a, b, (((1,), (1,)), ((), ())), preferred_element_type=F32)


def mm_tn(a, b):
    return lax.dot_general(a, b, (((0,), (0,)), ((), ())), preferred_element_type=F32)


def normalize(x):
    center = x - jnp.mean(x, -1, keepdims=True)
    rstd = lax.rsqrt(jnp.mean(center * center, -1, keepdims=True) + epsilon)
    return center * rstd, rstd


def norm_back(dh, gain, xhat, rstd):
    dxhat = dh * gain
    a = jnp.mean(dxhat, -1, keepdims=True)
    b = jnp.mean(dxhat * xhat, -1, keepdims=True)
    return rstd * (dxhat - a - xhat * b)


def rotate(block, cosine, sine):
    a, b = block[:HALF], block[HALF:]
    return jnp.concatenate([a * cosine - b * sine, b * cosine + a * sine], 0)


def qkv_kernel(place, tok, gain, bias, wq, wk, wv, cosine, sine, out, normed):
    xhat, _ = normalize(tok[...].astype(F32))
    normed[...] = xhat.astype(BF)
    h1 = (xhat * gain[...] + bias[...]).astype(BF)
    cos = jnp.concatenate([cosine[...]] * 2, 1)
    sin = jnp.concatenate([sine[...]] * 2, 1)
    for n, w in enumerate((wq, wk, wv)):
        t = mm(h1, w[...]).T
        for h in range(HEADS):
            block = t[h * HEAD_DIM : (h + 1) * HEAD_DIM]
            if n < 2:
                block = rotate(block, cos, sin)
            block = block.astype(BF)
            for k in range(2):
                out[h, k, n * HEAD_DIM : (n + 1) * HEAD_DIM, :] = block[:, k * 128 : (k + 1) * 128]


def whole(*shape):
    return pl.BlockSpec(shape, lambda *_: (0,) * len(shape))


def qkv_call(place, tok, gain, bias, wq, wk, wv, cos, sin):
    rows, width = tok.shape
    table = pl.BlockSpec((HALF, 128), lambda i, p: (0, p[0]))
    return pl.pallas_call(
        qkv_kernel,
        grid_spec=pltpu.PrefetchScalarGridSpec(
            num_scalar_prefetch=1,
            grid=(1,),
            in_specs=[whole(rows, width)]
            + [whole(1, width)] * 2
            + [whole(width, width)] * 3
            + [table, table],
            out_specs=(whole(HEADS, 2, PARTS, 128), whole(rows, width)),
        ),
        out_shape=(
            jax.ShapeDtypeStruct((HEADS, 2, PARTS, 128), BF),
            jax.ShapeDtypeStruct((rows, width), BF),
        ),
        compiler_params=pltpu.CompilerParams(vmem_limit_bytes=VMEM_LIMIT),
        name="qkv_forward",
    )(place, tok, gain, bias, wq, wk, wv, cos, sin)


def gather_rows(ref, w, lo, n):
    return jnp.concatenate([ref[s, w, lo : lo + n, :] for s in range(HEADS)], axis=1)


def split2(x):
    hi = x.astype(BF)
    return hi, (x - hi.astype(F32)).astype(BF)


def split3(x):
    hi = x.astype(BF)
    rest = x - hi.astype(F32)
    mid = rest.astype(BF)
    return hi, mid, (rest - mid.astype(F32)).astype(BF)


def key_rows(kt, length):
    place = lax.broadcasted_iota(jnp.int32, (16, LENGTH), 1)
    row = lax.broadcasted_iota(jnp.int32, (16, LENGTH), 0)
    mask = jnp.where(place < length, 0.0, masked_score)
    extra = jnp.where(row == 0, mask, jnp.where(row < 4, 1.0, 0.0)).astype(BF)
    zeros = jnp.zeros((48, LENGTH), BF)
    return jnp.concatenate([kt, kt, extra, zeros], 0).T


TQ = 256


def attend_kernel(lengths, qkv, out, mixed, total, kaug, qaug, vaug):
    for w in range(2):
        kt = gather_rows(qkv, w, 32, 32)
        kaug[...] = key_rows(kt, lengths[w])
        qs = gather_rows(qkv, w, 0, 32).astype(F32) * score_scale
        hi, lo = split2(qs)
        row = lax.broadcasted_iota(jnp.int32, (64, LENGTH), 0)
        qaug[...] = jnp.concatenate([hi, lo, jnp.where(row == 0, 1.0, 0.0).astype(BF)], 0)
        row = lax.broadcasted_iota(jnp.int32, (16, LENGTH), 0)
        vaug[...] = jnp.concatenate(
            [gather_rows(qkv, w, 64, 32), jnp.where(row == 0, 1.0, 0.0).astype(BF)], 0
        )

        def tile(t, carry):
            cols = pl.ds(pl.multiple_of(t * TQ, TQ), TQ)
            st = mm(kaug[...], qaug[:, cols])
            peak = jnp.max(st, 0, keepdims=True)
            p = jnp.exp2(st - peak).astype(BF)
            o = mm(vaug[...], p)
            norm = o[32:33]
            ot = o[:32] / norm
            mixed[w, :, cols] = ot
            total[w, :, cols] = peak + jnp.log2(norm)
            for j in range(TQ // 128):
                out[t * (TQ // 128) + j, w] = ot[:, j * 128 : (j + 1) * 128].astype(BF)
            return carry

        lax.fori_loop(0, LENGTH // TQ, tile, 0)


SMEM = pl.BlockSpec(memory_space=pltpu.SMEM)
VM = pl.BlockSpec(memory_space=pltpu.VMEM)


def attend_call(lengths, qkv):
    return pl.pallas_call(
        attend_kernel,
        out_shape=(
            jax.ShapeDtypeStruct((HEADS, 2, HEAD_DIM, 128), BF),
            jax.ShapeDtypeStruct((2, HEAD_DIM, LENGTH), F32),
            jax.ShapeDtypeStruct((2, 1, LENGTH), F32),
        ),
        in_specs=[SMEM, VM],
        out_specs=(VM, VM, VM),
        scratch_shapes=[
            pltpu.VMEM((LENGTH, 128), BF),
            pltpu.VMEM((128, LENGTH), BF),
            pltpu.VMEM((48, LENGTH), BF),
        ],
        compiler_params=pltpu.CompilerParams(vmem_limit_bytes=VMEM_LIMIT),
        name="attend_forward",
    )(lengths, qkv)


def attend_back_kernel(
    lengths, qkv, dot_in, mixed, total, cosine, sine, normed, wt, gain, bias, vec_in,
    out, grads, kaug, qaug, vaug, doaug, right, dkv, dqs,
):
    projected = None
    sums = None
    for w in range(2):
        kt = gather_rows(qkv, w, 32, 32)
        kaug[...] = key_rows(kt, lengths[w])
        qt = gather_rows(qkv, w, 0, 32)
        hi, lo = split2(qt.astype(F32) * score_scale)
        row = lax.broadcasted_iota(jnp.int32, (16, LENGTH), 0)

        def rows_of(first, second, third, fourth):
            return jnp.where(
                row == 0,
                first,
                jnp.where(
                    row == 1, second, jnp.where(row == 2, third, jnp.where(row == 3, fourth, 0.0))
                ),
            ).astype(BF)

        l1, l2, l3 = (v.astype(F32) for v in split3(-total[w]))
        qaug[...] = jnp.concatenate(
            [hi, lo, rows_of(1.0, l1, l2, l3), jnp.zeros((48, LENGTH), BF)], 0
        )
        do = gather_rows(dot_in, w, 0, 32)
        delta = jnp.sum(do.astype(F32) * mixed[w], 0, keepdims=True)
        d1, d2, d3 = (v.astype(F32) for v in split3(-delta))
        doaug[...] = jnp.concatenate(
            [do, rows_of(d1, d2, d3, 0.0), jnp.zeros((80, LENGTH), BF)], 0
        )
        vaug[...] = jnp.concatenate(
            [
                gather_rows(qkv, w, 64, 32),
                jnp.where(row < 3, 1.0, 0.0).astype(BF),
                jnp.zeros((80, LENGTH), BF),
            ],
            0,
        ).T
        right[...] = jnp.concatenate([qt, do, jnp.zeros((64, LENGTH), BF)], 0).T
        dkv[...] = jnp.zeros_like(dkv)
        lane = lax.broadcasted_iota(jnp.int32, (TQ, 128), 1)

        def tile(t, carry):
            cols = pl.ds(pl.multiple_of(t * TQ, TQ), TQ)
            st = mm(kaug[...], qaug[:, cols])
            probs = jnp.exp2(st)
            ds = (probs * mm(vaug[...], doaug[:, cols])).astype(BF)
            both = jnp.concatenate([ds, probs.astype(BF)], 1)
            r = right[cols, :]
            zero = jnp.zeros_like(r)
            pair = jnp.concatenate(
                [jnp.where(lane < 32, r, zero), jnp.where(lane < 32, zero, r)], 0
            )
            dkv[...] += mm(both, pair)
            dq = mm(kt, ds) * inv_root
            dq = rotate(dq, cosine[:, cols], -sine[:, cols])
            dq = dq.astype(BF)
            dqs[:, cols] = dq
            for j in range(TQ // 128):
                out[t * (TQ // 128) + j, w, 0:32, :] = dq[:, j * 128 : (j + 1) * 128]
            return carry

        lax.fori_loop(0, LENGTH // TQ, tile, 0)
        back = dkv[...].T
        dk = rotate(back[:32] * inv_root, cosine[...], -sine[...]).astype(BF)
        dv = back[32:64].astype(BF)
        for s in range(HEADS):
            out[s, w, 32:64, :] = dk[:, s * 128 : (s + 1) * 128]
            out[s, w, 64:96, :] = dv[:, s * 128 : (s + 1) * 128]
        d = jnp.concatenate([dqs[...], dk, dv], 0)
        x = jnp.concatenate([normed[s, w * 128 : (w + 1) * 128, :] for s in range(HEADS)], 0)
        part = mm(d, x)
        part_sum = jnp.sum(d.astype(F32), 1, keepdims=True)
        projected = part if w == 0 else projected + part
        sums = part_sum if w == 0 else sums + part_sum
    columns = wt[...].astype(F32)
    grads[0:PARTS] = (projected * gain[...] + sums * bias[...]).astype(BF)
    row = lax.broadcasted_iota(jnp.int32, (32, 512), 0)
    dgain = jnp.sum(columns * projected, 0, keepdims=True)
    dbias = jnp.sum(columns * sums, 0, keepdims=True)
    tail = jnp.where(
        row == 0,
        dgain,
        jnp.where(
            row == 1,
            dbias,
            jnp.where(row == 2, vec_in[0:1], jnp.where(row == 3, vec_in[1:2], 0.0)),
        ),
    )
    grads[PARTS:128] = tail.astype(BF)


def attend_back_call(lengths, qkv, do, mixed, total, cos, sin, normed, wt, gain, bias, vecs):
    return pl.pallas_call(
        attend_back_kernel,
        out_shape=(
            jax.ShapeDtypeStruct((HEADS, 2, PARTS, 128), BF),
            jax.ShapeDtypeStruct((128, 512), BF),
        ),
        in_specs=[SMEM] + [VM] * 11,
        out_specs=(VM, VM),
        scratch_shapes=[
            pltpu.VMEM((LENGTH, 128), BF),
            pltpu.VMEM((128, LENGTH), BF),
            pltpu.VMEM((LENGTH, 128), BF),
            pltpu.VMEM((128, LENGTH), BF),
            pltpu.VMEM((LENGTH, 128), BF),
            pltpu.VMEM((LENGTH, 128), F32),
            pltpu.VMEM((32, LENGTH), BF),
        ],
        compiler_params=pltpu.CompilerParams(vmem_limit_bytes=VMEM_LIMIT),
        name="attend_backward",
    )(lengths, qkv, do, mixed, total, cos, sin, normed, wt, gain, bias, vecs)


FC = 512


def ff_kernel(
    tok, ob, wout, gain, bias, wg, wu, wd, cot,
    output, gwg, gwu, gwd, gwout, vecs, dres, dot_out,
    res, h2, h2t, dh2, obt,
):
    step = pl.program_id(0)
    last = pl.num_programs(0) - 1

    @pl.when(step == 0)
    def first():
        for k in range(2):
            obt[:, k * 128 : (k + 1) * 128] = ob[:, k].reshape(512, 128)
        r = tok[...].astype(F32) + mm(obt[...].T, wout[...])
        xhat, _ = normalize(r)
        h = (xhat * gain[...] + bias[...]).astype(BF)
        res[...] = r
        h2[...] = h
        h2t[...] = h.T
        output[...] = r
        dh2[...] = jnp.zeros_like(dh2)

    gate = mm(h2[...], wg[...])
    up = mm(h2[...], wu[...])
    dm = mm_nt(cot[...], wd[...])
    sg = jax.nn.sigmoid(gate)
    act = gate * sg
    m = (act * up).astype(BF)
    dgate = (dm * up * (sg * (1.0 + gate - act))).astype(BF)
    dup = (dm * act).astype(BF)
    output[...] += mm(m, wd[...])
    gwd[...] = mm(m.T, cot[...])
    gwg[...] = mm(h2t[...], dgate)
    gwu[...] = mm(h2t[...], dup)
    dh2[...] += mm_nt(dgate, wg[...]) + mm_nt(dup, wu[...])

    @pl.when(step == last)
    def final():
        xhat, rstd = normalize(res[...])
        dh = dh2[...]
        vecs[0:1] = jnp.sum(dh * xhat, 0, keepdims=True)
        vecs[1:2] = jnp.sum(dh, 0, keepdims=True)
        dr = cot[...].astype(F32) + norm_back(dh, gain[...], xhat, rstd)
        dres[...] = dr
        da = dr.astype(BF)
        gwout[...] = mm(obt[...], da)
        do = mm_nt(wout[...], da).astype(BF)
        for k in range(2):
            dot_out[:, k] = do[:, k * 128 : (k + 1) * 128].reshape(HEADS, HEAD_DIM, 128)


def ff_call(tok, ob, wout, gain, bias, wg, wu, wd, cot):
    rows, width = tok.shape
    ff = wg.shape[1]

    return pl.pallas_call(
        ff_kernel,
        grid=(ff // FC,),
        in_specs=[
            whole(rows, width),
            whole(HEADS, 2, HEAD_DIM, 128),
            whole(width, width),
            whole(1, width),
            whole(1, width),
            pl.BlockSpec((width, FC), lambda i: (0, i)),
            pl.BlockSpec((width, FC), lambda i: (0, i)),
            pl.BlockSpec((FC, width), lambda i: (i, 0)),
            whole(rows, width),
        ],
        out_specs=(
            whole(rows, width),
            pl.BlockSpec((width, FC), lambda i: (0, i)),
            pl.BlockSpec((width, FC), lambda i: (0, i)),
            pl.BlockSpec((FC, width), lambda i: (i, 0)),
            whole(width, width),
            whole(2, width),
            whole(rows, width),
            whole(HEADS, 2, HEAD_DIM, 128),
        ),
        out_shape=(
            jax.ShapeDtypeStruct((rows, width), F32),
            jax.ShapeDtypeStruct((width, ff), F32),
            jax.ShapeDtypeStruct((width, ff), F32),
            jax.ShapeDtypeStruct((ff, width), F32),
            jax.ShapeDtypeStruct((width, width), F32),
            jax.ShapeDtypeStruct((2, width), F32),
            jax.ShapeDtypeStruct((rows, width), F32),
            jax.ShapeDtypeStruct((HEADS, 2, HEAD_DIM, 128), BF),
        ),
        scratch_shapes=[
            pltpu.VMEM((rows, width), F32),
            pltpu.VMEM((rows, width), BF),
            pltpu.VMEM((width, rows), BF),
            pltpu.VMEM((rows, width), F32),
            pltpu.VMEM((width, rows), BF),
        ],
        compiler_params=pltpu.CompilerParams(vmem_limit_bytes=VMEM_LIMIT),
        name="feed_forward",
    )(tok, ob, wout, gain, bias, wg, wu, wd, cot)


def proj_back_kernel(tok, dres, dqkv, wq, wk, wv, gain, gtok):
    xhat, rstd = normalize(tok[...].astype(F32))
    total = None
    for n, w in enumerate((wq, wk, wv)):
        lo = n * HEAD_DIM
        d = jnp.concatenate(
            [dqkv[:, k, lo : lo + HEAD_DIM, :].reshape(512, 128) for k in range(2)], 1
        )
        part = mm(w[...], d)
        total = part if total is None else total + part
    gtok[...] = dres[...] + norm_back(total.T, gain[...], xhat, rstd)


def proj_back_call(tok, dres, dqkv, wq, wk, wv, gain):
    rows, width = tok.shape
    return pl.pallas_call(
        proj_back_kernel,
        out_shape=jax.ShapeDtypeStruct((rows, width), F32),
        compiler_params=pltpu.CompilerParams(vmem_limit_bytes=VMEM_LIMIT),
        name="projection_backward",
    )(tok, dres, dqkv, wq, wk, wv, gain)


def unpack_kernel(core, mine, other, gwq, gwk, gwv, vecs):
    first = core[0] == 0
    even = jnp.where(first, mine[...], other[...])
    odd = jnp.where(first, other[...], mine[...])
    for n, g in enumerate((gwq, gwk, gwv)):
        lo = n * HEAD_DIM
        rows = []
        for i in range(HEADS // 2):
            rows += [even[i, lo : lo + HEAD_DIM], odd[i, lo : lo + HEAD_DIM]]
        g[...] = jnp.concatenate(rows, 0).astype(F32).T
    total = even[0, PARTS:128].astype(F32) + odd[0, PARTS:128].astype(F32)
    for i in range(1, HEADS // 2):
        total += even[i, PARTS:128].astype(F32) + odd[i, PARTS:128].astype(F32)
    vecs[...] = total[:8]


def unpack_call(core, mine, other):
    width = mine.shape[-1]
    square = jax.ShapeDtypeStruct((width, width), F32)
    return pl.pallas_call(
        unpack_kernel,
        out_shape=(square, square, square, jax.ShapeDtypeStruct((8, width), F32)),
        in_specs=[SMEM, VM, VM],
        out_specs=(VM, VM, VM, VM),
        compiler_params=pltpu.CompilerParams(vmem_limit_bytes=VMEM_LIMIT),
        name="unpack_projections",
    )(core, mine, other)


def angles():
    inverse = np.float32(10000.0) ** (-np.arange(HALF, dtype=np.float32) * np.float32(2.0 / HEAD_DIM))
    turn = inverse[:, None] * np.arange(LENGTH, dtype=np.float32)[None, :]
    turn = turn.astype(np.float64)
    return np.cos(turn).astype(np.float32), np.sin(turn).astype(np.float32)


SEQ = ("x", "zh", "c")
WIN = ("y", "zl")
CHIPS = ("x", "zh")


def exchange(x, axes):
    return lax.all_to_all(x, axes, 0, 0, tiled=True)


def spread(x, axes, n):
    return exchange(jnp.broadcast_to(x[None], (n,) + x.shape), axes)


def local(
    tokens, lengths, gain_one, bias_one, weight_query, weight_key, weight_value, weight_out,
    gain_two, bias_two, weight_gate, weight_up, weight_down, cotangent,
):
    win_count, seq_rows, width = tokens.shape
    rows = win_count * seq_rows
    tok = tokens.reshape(rows, width)
    cot = cotangent.reshape(rows, width)
    g1, b1, g2, b2 = (v.reshape(1, width) for v in (gain_one, bias_one, gain_two, bias_two))
    cos, sin = angles()
    head = lax.axis_index(SEQ)
    core = lax.axis_index("c").reshape(1)
    columns = jnp.concatenate(
        [
            lax.dynamic_slice_in_dim(w, head * HEAD_DIM, HEAD_DIM, 1)
            for w in (weight_query, weight_key, weight_value)
        ],
        1,
    ).T

    sent, normed = qkv_call(
        head.reshape(1), tok, g1, b1, weight_query, weight_key, weight_value, cos, sin
    )
    qkv = exchange(sent, SEQ)
    normed = lax.all_gather(normed, SEQ, axis=0)
    mixed_low, mixed, total = attend_call(lengths, qkv)
    ob = exchange(mixed_low, SEQ)
    output, gwg, gwu, gwd, gwout, vecs, dres, dot_out = ff_call(
        tok, ob, weight_out, g2, b2, weight_gate, weight_up, weight_down, cot
    )
    gwg, gwu, gwd, gwout = lax.psum((gwg, gwu, gwd, gwout), SEQ + WIN)
    do = exchange(dot_out, SEQ)
    dqkv, grads = attend_back_call(
        lengths, qkv, do, mixed, total, cos, sin, normed, columns, g1, b1, vecs
    )
    dqkv = exchange(dqkv, SEQ)
    gtok = proj_back_call(tok, dres, dqkv, weight_query, weight_key, weight_value, g1)
    parts = exchange(grads.reshape(8, 16, width), WIN)
    part = jnp.sum(parts.astype(F32), 0).astype(BF)
    grads = spread(part, WIN, 8).reshape(128, width)
    mine = spread(grads, CHIPS, 8)
    other = lax.ppermute(mine, "c", [(0, 1), (1, 0)])
    gwq, gwk, gwv, vecs = unpack_call(core, mine, other)
    return (
        output.reshape(tokens.shape),
        gtok.reshape(tokens.shape),
        vecs[0],
        vecs[1],
        gwq,
        gwk,
        gwv,
        gwout,
        vecs[2],
        vecs[3],
        gwg,
        gwu,
        gwd,
    )


def solution(mesh):
    fine = Mesh(mesh.devices.reshape(4, 2, 2, 4, 2), SEQ + WIN)
    sharded = P(WIN, SEQ, None)
    return jax.shard_map(
        local,
        mesh=fine,
        in_specs=(sharded, P(WIN)) + (P(),) * 11 + (sharded,),
        out_specs=(sharded, sharded) + (P(),) * 11,
        check_vma=False,
    )
```

```python
import functools
import math

import jax
import jax.numpy as jnp
import numpy as np
from jax import lax
from jax.experimental import pallas as pl
from jax.experimental.pallas import tpu as pltpu
from jax.sharding import Mesh
from jax.sharding import PartitionSpec as P

HEADS = 16
HEAD_DIM = 32
HALF = HEAD_DIM // 2
PARTS = 3 * HEAD_DIM
LENGTH = 2048
epsilon = 1e-05
masked_score = -1e30
BF = jnp.bfloat16
F32 = jnp.float32
inv_root = HEAD_DIM ** (-0.5)
score_scale = inv_root * math.log2(math.e)
VMEM_LIMIT = 60 * 1024 * 1024


def cost(flops, nbytes=1 << 20):
    return pl.CostEstimate(flops=flops, bytes_accessed=nbytes, transcendentals=0)


def mm(a, b):
    return jnp.dot(a, b, preferred_element_type=F32)


def mm_nt(a, b):
    return lax.dot_general(a, b, (((1,), (1,)), ((), ())), preferred_element_type=F32)


def mm_tn(a, b):
    return lax.dot_general(a, b, (((0,), (0,)), ((), ())), preferred_element_type=F32)


def normalize(x):
    center = x - jnp.mean(x, -1, keepdims=True)
    rstd = lax.rsqrt(jnp.mean(center * center, -1, keepdims=True) + epsilon)
    return center * rstd, rstd


def norm_back(dh, gain, xhat, rstd):
    dxhat = dh * gain
    a = jnp.mean(dxhat, -1, keepdims=True)
    b = jnp.mean(dxhat * xhat, -1, keepdims=True)
    return rstd * (dxhat - a - xhat * b)


def rotate(block, cosine, sine):
    a, b = block[:HALF], block[HALF:]
    return jnp.concatenate([a * cosine - b * sine, b * cosine + a * sine], 0)


def head_of(number):
    return number // 8


def core_of(number):
    return number // 8 % 2


def y_of(number):
    return number // 2 % 4


def qkv_kernel(place, tok, gain, bias, wq, wk, wv, cosine, sine, out):
    xhat, _ = normalize(tok[...].astype(F32))
    h1 = (xhat * gain[...] + bias[...]).astype(BF)
    cos = jnp.concatenate([cosine[...]] * 2, 1)
    sin = jnp.concatenate([sine[...]] * 2, 1)
    for n, w in enumerate((wq, wk, wv)):
        t = mm(h1, w[...]).T
        for h in range(HEADS):
            block = t[h * HEAD_DIM : (h + 1) * HEAD_DIM]
            if n < 2:
                block = rotate(block, cos, sin)
            block = block.astype(BF)
            for k in range(2):
                out[h, k, n * HEAD_DIM : (n + 1) * HEAD_DIM, :] = block[:, k * 128 : (k + 1) * 128]


def whole(*shape):
    return pl.BlockSpec(shape, lambda *_: (0,) * len(shape))


def qkv_call(place, tok, gain, bias, wq, wk, wv, cos, sin):
    rows, width = tok.shape
    table = pl.BlockSpec((HALF, 128), lambda i, p: (0, head_of(p[0])))
    return pl.pallas_call(
        qkv_kernel,
        grid_spec=pltpu.PrefetchScalarGridSpec(
            num_scalar_prefetch=1,
            grid=(1,),
            in_specs=[whole(rows, width)]
            + [whole(1, width)] * 2
            + [whole(width, width)] * 3
            + [table, table],
            out_specs=whole(HEADS, 2, PARTS, 128),
        ),
        out_shape=jax.ShapeDtypeStruct((HEADS, 2, PARTS, 128), BF),
        cost_estimate=cost(2 * rows * width * width * 3),
        compiler_params=pltpu.CompilerParams(vmem_limit_bytes=VMEM_LIMIT),
        name="qkv_forward",
    )(place, tok, gain, bias, wq, wk, wv, cos, sin)


def gather_rows(ref, w, lo, n):
    return jnp.concatenate([ref[s, w, lo : lo + n, :] for s in range(HEADS)], axis=1)


def split2(x):
    hi = x.astype(BF)
    return hi, (x - hi.astype(F32)).astype(BF)


def split3(x):
    hi = x.astype(BF)
    rest = x - hi.astype(F32)
    mid = rest.astype(BF)
    return hi, mid, (rest - mid.astype(F32)).astype(BF)


def key_rows(kt, length):
    place = lax.broadcasted_iota(jnp.int32, (16, LENGTH), 1)
    row = lax.broadcasted_iota(jnp.int32, (16, LENGTH), 0)
    mask = jnp.where(place < length, 0.0, masked_score)
    extra = jnp.where(row == 0, mask, jnp.where(row < 4, 1.0, 0.0)).astype(BF)
    zeros = jnp.zeros((48, LENGTH), BF)
    return jnp.concatenate([kt, kt, extra, zeros], 0).T


TQ = 1024
TB = 512


def attend_kernel(lengths, qkv, out, mixed, total, kaug, qaug, vaug):
    for w in range(2):
        kt = gather_rows(qkv, w, 32, 32)
        kaug[...] = key_rows(kt, lengths[w])
        qs = gather_rows(qkv, w, 0, 32).astype(F32) * score_scale
        hi, lo = split2(qs)
        row = lax.broadcasted_iota(jnp.int32, (64, LENGTH), 0)
        qaug[...] = jnp.concatenate([hi, lo, jnp.where(row == 0, 1.0, 0.0).astype(BF)], 0)
        row = lax.broadcasted_iota(jnp.int32, (16, LENGTH), 0)
        vaug[...] = jnp.concatenate(
            [gather_rows(qkv, w, 64, 32), jnp.where(row == 0, 1.0, 0.0).astype(BF)], 0
        )

        def tile(t, carry):
            cols = pl.ds(pl.multiple_of(t * TQ, TQ), TQ)
            st = mm(kaug[...], qaug[:, cols])
            peak = jnp.max(st, 0, keepdims=True)
            p = jnp.exp2(st - peak).astype(BF)
            o = mm(vaug[...], p)
            norm = o[32:33]
            ot = o[:32] / norm
            mixed[w, :, cols] = ot
            total[w, :, cols] = peak + jnp.log2(norm)
            for j in range(TQ // 128):
                out[t * (TQ // 128) + j, w] = ot[:, j * 128 : (j + 1) * 128].astype(BF)
            return carry

        lax.fori_loop(0, LENGTH // TQ, tile, 0)


SMEM = pl.BlockSpec(memory_space=pltpu.SMEM)
VM = pl.BlockSpec(memory_space=pltpu.VMEM)


def attend_call(lengths, qkv):
    return pl.pallas_call(
        attend_kernel,
        out_shape=(
            jax.ShapeDtypeStruct((HEADS, 2, HEAD_DIM, 128), BF),
            jax.ShapeDtypeStruct((2, HEAD_DIM, LENGTH), F32),
            jax.ShapeDtypeStruct((2, 1, LENGTH), F32),
        ),
        in_specs=[SMEM, VM],
        out_specs=(VM, VM, VM),
        scratch_shapes=[
            pltpu.VMEM((LENGTH, 128), BF),
            pltpu.VMEM((128, LENGTH), BF),
            pltpu.VMEM((48, LENGTH), BF),
        ],
        cost_estimate=cost(1 << 34),
        compiler_params=pltpu.CompilerParams(vmem_limit_bytes=VMEM_LIMIT),
        name="attend_forward",
    )(lengths, qkv)


def attend_back_kernel(
    lengths, qkv, dot_in, mixed, total, cosine, sine, out, kaug, qaug, vaug, doaug, right, dkv
):
    for w in range(2):
        kt = gather_rows(qkv, w, 32, 32)
        kaug[...] = key_rows(kt, lengths[w])
        qt = gather_rows(qkv, w, 0, 32)
        hi, lo = split2(qt.astype(F32) * score_scale)
        row = lax.broadcasted_iota(jnp.int32, (16, LENGTH), 0)

        def rows_of(first, second, third, fourth):
            return jnp.where(
                row == 0,
                first,
                jnp.where(
                    row == 1, second, jnp.where(row == 2, third, jnp.where(row == 3, fourth, 0.0))
                ),
            ).astype(BF)

        l1, l2, l3 = (v.astype(F32) for v in split3(-total[w]))
        qaug[...] = jnp.concatenate(
            [hi, lo, rows_of(1.0, l1, l2, l3), jnp.zeros((48, LENGTH), BF)], 0
        )
        do = gather_rows(dot_in, w, 0, 32)
        delta = jnp.sum(do.astype(F32) * mixed[w], 0, keepdims=True)
        d1, d2, d3 = (v.astype(F32) for v in split3(-delta))
        doaug[...] = jnp.concatenate(
            [do, rows_of(d1, d2, d3, 0.0), jnp.zeros((80, LENGTH), BF)], 0
        )
        vaug[...] = jnp.concatenate(
            [
                gather_rows(qkv, w, 64, 32),
                jnp.where(row < 3, 1.0, 0.0).astype(BF),
                jnp.zeros((80, LENGTH), BF),
            ],
            0,
        ).T
        right[...] = jnp.concatenate([qt, do, jnp.zeros((64, LENGTH), BF)], 0).T
        dkv[...] = jnp.zeros_like(dkv)
        lane = lax.broadcasted_iota(jnp.int32, (TB, 128), 1)

        def tile(t, carry):
            cols = pl.ds(pl.multiple_of(t * TB, TB), TB)
            st = mm(kaug[...], qaug[:, cols])
            probs = jnp.exp2(st)
            ds = (probs * mm(vaug[...], doaug[:, cols])).astype(BF)
            both = jnp.concatenate([ds, probs.astype(BF)], 1)
            r = right[cols, :]
            zero = jnp.zeros_like(r)
            pair = jnp.concatenate(
                [jnp.where(lane < 32, r, zero), jnp.where(lane < 32, zero, r)], 0
            )
            dkv[...] += mm(both, pair)
            dq = mm(kt, ds) * inv_root
            dq = rotate(dq, cosine[:, cols], -sine[:, cols])
            dq = dq.astype(BF)
            for j in range(TB // 128):
                out[t * (TB // 128) + j, w, 0:32, :] = dq[:, j * 128 : (j + 1) * 128]
            return carry

        lax.fori_loop(0, LENGTH // TB, tile, 0)
        back = dkv[...].T
        dk = rotate(back[:32] * inv_root, cosine[...], -sine[...]).astype(BF)
        dv = back[32:64].astype(BF)
        for s in range(HEADS):
            out[s, w, 32:64, :] = dk[:, s * 128 : (s + 1) * 128]
            out[s, w, 64:96, :] = dv[:, s * 128 : (s + 1) * 128]


def attend_back_call(lengths, qkv, do, mixed, total, cos, sin):
    return pl.pallas_call(
        attend_back_kernel,
        out_shape=jax.ShapeDtypeStruct((HEADS, 2, PARTS, 128), BF),
        in_specs=[SMEM] + [VM] * 6,
        out_specs=VM,
        scratch_shapes=[
            pltpu.VMEM((LENGTH, 128), BF),
            pltpu.VMEM((128, LENGTH), BF),
            pltpu.VMEM((LENGTH, 128), BF),
            pltpu.VMEM((128, LENGTH), BF),
            pltpu.VMEM((LENGTH, 128), BF),
            pltpu.VMEM((LENGTH, 128), F32),
        ],
        cost_estimate=cost(1 << 34),
        compiler_params=pltpu.CompilerParams(vmem_limit_bytes=VMEM_LIMIT),
        name="attend_backward",
    )(lengths, qkv, do, mixed, total, cos, sin)


def ordered(ref, core, y):
    rows = []
    for o in range(2):
        for d in range(4):
            start = (core + o) % 2 * 256 + (y + d) % 4 * 64
            rows.append(ref[pl.ds(pl.multiple_of(start, 64), 64), :])
    return jnp.concatenate(rows, 0)


def pack(refs, index, value):
    for o in range(2):
        for d in range(4):
            for j in range(4):
                for l in range(4):
                    lo = o * 256 + d * 64 + j * 16
                    refs[o * 4 + d][(4 * j + l,) + index] = value[
                        lo : lo + 16, l * 128 : (l + 1) * 128
                    ].astype(BF)


def unpack(ref, index, out, where):
    for j in range(4):
        for l in range(4):
            out[where + (slice(j * 16, j * 16 + 16), slice(l * 128, l * 128 + 128))] = ref[
                (4 * j + l,) + index
            ].astype(F32)


FC = 512


def ff_kernel(
    place, tok, ob, wout, gain, bias, wg, wu, wd, cot,
    output, k0, k1, k2, k3, s0, s1, s2, s3, gwout, vecs, dres, dot_out,
    res, h2, h2t, dh2, obt, mt,
):
    pieces = (k0, k1, k2, k3, s0, s1, s2, s3)
    core, y = core_of(place[0]), y_of(place[0])
    step = pl.program_id(0)
    last = pl.num_programs(0) - 1

    @pl.when(step == 0)
    def first():
        for k in range(2):
            obt[:, k * 128 : (k + 1) * 128] = ob[:, k].reshape(512, 128)
        r = tok[...].astype(F32) + mm(obt[...].T, wout[...])
        xhat, _ = normalize(r)
        h = (xhat * gain[...] + bias[...]).astype(BF)
        res[...] = r
        h2[...] = h
        mt[...] = h.T
        h2t[...] = ordered(mt, core, y)
        output[...] = r
        dh2[...] = jnp.zeros_like(dh2)

    gate = mm(h2[...], wg[...])
    up = mm(h2[...], wu[...])
    dm = mm_nt(cot[...], wd[...])
    sg = jax.nn.sigmoid(gate)
    act = gate * sg
    m = (act * up).astype(BF)
    dgate = (dm * up * (sg * (1.0 + gate - act))).astype(BF)
    dup = (dm * act).astype(BF)
    output[...] += mm(m, wd[...])
    mt[...] = m.T
    pack(pieces, (0, 0), mm(h2t[...], dgate))
    pack(pieces, (1, 0), mm(h2t[...], dup))
    pack(pieces, (2, 0), mm(ordered(mt, core, y), cot[...]))
    dh2[...] += mm_nt(dgate, wg[...]) + mm_nt(dup, wu[...])

    @pl.when(step == last)
    def final():
        xhat, rstd = normalize(res[...])
        dh = dh2[...]
        vecs[0:1] = jnp.sum(dh * xhat, 0, keepdims=True)
        vecs[1:2] = jnp.sum(dh, 0, keepdims=True)
        dr = cot[...].astype(F32) + norm_back(dh, gain[...], xhat, rstd)
        dres[...] = dr
        da = dr.astype(BF)
        gwout[...] = mm(ordered(obt, core, y), da)
        do = mm_nt(wout[...], da).astype(BF)
        for k in range(2):
            dot_out[:, k] = do[:, k * 128 : (k + 1) * 128].reshape(HEADS, HEAD_DIM, 128)


def ff_call(place, tok, ob, wout, gain, bias, wg, wu, wd, cot):
    rows, width = tok.shape
    ff = wg.shape[1]

    return pl.pallas_call(
        ff_kernel,
        grid_spec=pltpu.PrefetchScalarGridSpec(
            num_scalar_prefetch=1,
            grid=(ff // FC,),
            in_specs=[
                whole(rows, width),
                whole(HEADS, 2, HEAD_DIM, 128),
                whole(width, width),
                whole(1, width),
                whole(1, width),
                pl.BlockSpec((width, FC), lambda i, c: (0, i)),
                pl.BlockSpec((width, FC), lambda i, c: (0, i)),
                pl.BlockSpec((FC, width), lambda i, c: (i, 0)),
                whole(rows, width),
            ],
            out_specs=(
                whole(rows, width),
            )
            + (pl.BlockSpec((16, 3, 1, 16, 128), lambda i, c: (0, 0, i, 0, 0)),) * 8
            + (
                whole(width, width),
                whole(2, width),
                whole(rows, width),
                whole(HEADS, 2, HEAD_DIM, 128),
            ),
            scratch_shapes=[
                pltpu.VMEM((rows, width), F32),
                pltpu.VMEM((rows, width), BF),
                pltpu.VMEM((width, rows), BF),
                pltpu.VMEM((rows, width), F32),
                pltpu.VMEM((width, rows), BF),
                pltpu.VMEM((FC, rows), BF),
            ],
        ),
        out_shape=(
            jax.ShapeDtypeStruct((rows, width), F32),
        )
        + (jax.ShapeDtypeStruct((16, 3, 4, 16, 128), BF),) * 8
        + (
            jax.ShapeDtypeStruct((width, width), F32),
            jax.ShapeDtypeStruct((2, width), F32),
            jax.ShapeDtypeStruct((rows, width), F32),
            jax.ShapeDtypeStruct((HEADS, 2, HEAD_DIM, 128), BF),
        ),
        cost_estimate=cost(2 * rows * width * ff * 9),
        compiler_params=pltpu.CompilerParams(vmem_limit_bytes=VMEM_LIMIT),
        name="feed_forward",
    )(place, tok, ob, wout, gain, bias, wg, wu, wd, cot)


def proj_back_kernel(place, tok, dres, dqkv, wq, wk, wv, gain, bias, gwout, vecs, gtok, *rest):
    pieces, h1t = rest[:8], rest[8]
    xhat, rstd = normalize(tok[...].astype(F32))
    h1t[...] = (xhat * gain[...] + bias[...]).astype(BF).T
    h = ordered(h1t, core_of(place[0]), y_of(place[0]))
    total = None
    for n, w in enumerate((wq, wk, wv)):
        lo = n * HEAD_DIM
        d = jnp.concatenate(
            [dqkv[:, k, lo : lo + HEAD_DIM, :].reshape(512, 128) for k in range(2)], 1
        )
        part = mm(w[...], d)
        total = part if total is None else total + part
        pack(pieces, (n,), mm_nt(h, d))
    pack(pieces, (3,), gwout[...])
    dh = total.T
    four = jnp.concatenate(
        [jnp.sum(dh * xhat, 0, keepdims=True), jnp.sum(dh, 0, keepdims=True), vecs[...]], 0
    )
    block = jnp.concatenate([four[:, l * 128 : (l + 1) * 128] for l in range(4)], 0).astype(BF)
    for ref in pieces:
        for j in range(16):
            ref[j, 4] = block
    gtok[...] = dres[...] + norm_back(dh, gain[...], xhat, rstd)


def proj_back_call(place, tok, dres, dqkv, wq, wk, wv, gain, bias, gwout, vecs):
    rows, width = tok.shape
    piece = jax.ShapeDtypeStruct((16, 5, 16, 128), BF)
    return pl.pallas_call(
        proj_back_kernel,
        out_shape=(jax.ShapeDtypeStruct((rows, width), F32),) + (piece,) * 8,
        in_specs=[SMEM] + [VM] * 10,
        out_specs=(VM,) * 9,
        scratch_shapes=[pltpu.VMEM((width, rows), BF)],
        cost_estimate=cost(2 * rows * width * width * 6),
        compiler_params=pltpu.CompilerParams(vmem_limit_bytes=VMEM_LIMIT),
        name="projection_backward",
    )(place, tok, dres, dqkv, wq, wk, wv, gain, bias, gwout, vecs)


def put_pieces(number, core, refs, write):
    for d, ref in enumerate(refs):
        write(ref, core, pl.multiple_of((y_of(number) + 4 - d) % 4 * 64, 64))


def wide_rows(ref, n, out, start):
    for j in range(4):
        rows = pl.ds(start + j * 16, 16)
        for i in range(4):
            for l in range(4):
                lo = i * 512 + l * 128
                out[0, rows, lo : lo + 128] = ref[4 * j + l, n, i].astype(F32)


def unpack_ff_kernel(place, *refs):
    gwg, gwu, gwd = refs[-3:]
    number = place[0]

    def write(ref, core, start):
        wide_rows(ref, 0, gwg, start)
        wide_rows(ref, 1, gwu, start)
        for j in range(4):
            rows = pl.ds(start + j * 16, 16)
            for i in range(4):
                for l in range(4):
                    gwd[i, 0, rows, l * 128 : (l + 1) * 128] = ref[4 * j + l, 2, i].astype(F32)

    put_pieces(number, None, refs[:4], write)


def unpack_ff_call(place, pieces, other, before):
    def spec(block, axis):
        def index(i, p):
            at = [0] * len(block)
            at[axis] = (core_of(p[0]) + other) % 2
            return tuple(at)

        return pl.BlockSpec(block, index)

    shapes = ((2, 256, 2048), (2, 256, 2048), (4, 2, 256, 512))
    return pl.pallas_call(
        unpack_ff_kernel,
        grid_spec=pltpu.PrefetchScalarGridSpec(
            num_scalar_prefetch=1,
            grid=(1,),
            in_specs=[whole(*pieces[0].shape)] * 4
            + [pl.BlockSpec(memory_space=pl.ANY)] * len(before),
            out_specs=(
                spec((1, 256, 2048), 0),
                spec((1, 256, 2048), 0),
                spec((4, 1, 256, 512), 1),
            ),
        ),
        out_shape=tuple(jax.ShapeDtypeStruct(shape, F32) for shape in shapes),
        input_output_aliases={5 + k: k for k in range(3)} if before else {},
        cost_estimate=cost(1 << 20, 9 << 20),
        compiler_params=pltpu.CompilerParams(vmem_limit_bytes=VMEM_LIMIT),
        name="unpack_feed_forward",
    )(place, *pieces, *before)


def unpack_kernel(place, *refs):
    outs = refs[-4:]
    number = place[0]

    def write(ref, core, start):
        for n, g in enumerate(outs):
            for j in range(4):
                rows = pl.ds(pl.multiple_of(core * 256 + start + j * 16, 16), 16)
                for l in range(4):
                    g[rows, l * 128 : (l + 1) * 128] = ref[4 * j + l, n].astype(F32)

    put_pieces(number, core_of(number), refs[:4], write)
    put_pieces(number, 1 - core_of(number), refs[4:8], write)


def unpack_call(place, mine, others):
    square = jax.ShapeDtypeStruct((512, 512), F32)
    return pl.pallas_call(
        unpack_kernel,
        out_shape=(square,) * 4,
        in_specs=[SMEM] + [VM] * 8,
        out_specs=(VM,) * 4,
        cost_estimate=cost(1 << 20, 6 << 20),
        compiler_params=pltpu.CompilerParams(vmem_limit_bytes=VMEM_LIMIT),
        name="unpack_projections",
    )(place, *mine, *others)


def angles():
    inverse = np.float32(10000.0) ** (-np.arange(HALF, dtype=np.float32) * np.float32(2.0 / HEAD_DIM))
    turn = inverse[:, None] * np.arange(LENGTH, dtype=np.float32)[None, :]
    turn = turn.astype(np.float64)
    return np.cos(turn).astype(np.float32), np.sin(turn).astype(np.float32)


SEQ = ("x", "zh", "c")
WIN = ("y", "zl")
REST = ("x", "zh", "zl")
SWAP = [(0, 1), (1, 0)]


def exchange(x, axes):
    return lax.all_to_all(x, axes, 0, 0, tiled=True)


def spread(x, axes, n):
    return exchange(jnp.broadcast_to(x[None], (n,) + x.shape), axes)


def add_up(*terms):
    return sum(t.astype(F32) for t in terms).astype(BF)


def along_y(x, d):
    return lax.ppermute(x, "y", [(i, (i + d) % 4) for i in range(4)])


def reduce_y(pieces):
    got = [lax.ppermute(p, "c", SWAP) for p in pieces[4:]]
    there = [along_y(add_up(pieces[d], got[d]), d) for d in (1, 2, 3)]
    return add_up(pieces[0], got[0], *there)


def reduce_rest(x):
    return jnp.sum(exchange(x, REST).astype(F32), 0).astype(BF)


def collect(whole_piece):
    mine = [whole_piece] + [along_y(whole_piece, d) for d in (1, 2, 3)]
    return mine, [lax.ppermute(m, "c", SWAP) for m in mine]


def after(x, *others):
    return lax.optimization_barrier((x,) + others)[0]


def local(
    tokens, lengths, gain_one, bias_one, weight_query, weight_key, weight_value, weight_out,
    gain_two, bias_two, weight_gate, weight_up, weight_down, cotangent,
):
    win_count, seq_rows, width = tokens.shape
    rows = win_count * seq_rows
    tok = tokens.reshape(rows, width)
    cot = cotangent.reshape(rows, width)
    g1, b1, g2, b2 = (v.reshape(1, width) for v in (gain_one, bias_one, gain_two, bias_two))
    cos, sin = angles()
    place = lax.axis_index(SEQ + WIN).reshape(1)

    sent = qkv_call(place, tok, g1, b1, weight_query, weight_key, weight_value, cos, sin)
    qkv = exchange(sent, SEQ)
    mixed_low, mixed, total = attend_call(lengths, qkv)
    ob = exchange(mixed_low, SEQ)
    output, *pieces, gwout, vecs, dres, dot_out = ff_call(
        place, tok, ob, weight_out, g2, b2, weight_gate, weight_up, weight_down, cot
    )
    do = exchange(dot_out, SEQ)
    ff = reduce_y(pieces)
    dqkv = exchange(attend_back_call(lengths, qkv, do, mixed, total, cos, sin), SEQ)
    ff = reduce_rest(after(ff, dqkv))
    gtok, *pieces = proj_back_call(
        place, tok, dres, dqkv, weight_query, weight_key, weight_value, g1, b1, gwout, vecs
    )
    ff = spread(ff, REST, 16)
    mine, others = collect(ff)
    gwg, gwu, gwd = unpack_ff_call(place, others, 1, unpack_ff_call(place, mine, 0, ()))
    part = reduce_rest(after(reduce_y(pieces), ff))
    four = part[4].reshape(4, 4, 128).transpose(1, 0, 2).reshape(4, width).astype(F32)
    gwq, gwk, gwv, gwout = unpack_call(place, *collect(spread(part[:4], REST, 16)))
    return (
        output.reshape(tokens.shape),
        gtok.reshape(tokens.shape),
        four[0],
        four[1],
        gwq,
        gwk,
        gwv,
        gwout,
        four[2],
        four[3],
        gwg.reshape(width, 2048),
        gwu.reshape(width, 2048),
        gwd.reshape(2048, width),
    )


def solution(mesh):
    fine = Mesh(mesh.devices.reshape(4, 2, 2, 4, 2), SEQ + WIN)
    sharded = P(WIN, SEQ, None)
    return jax.shard_map(
        local,
        mesh=fine,
        in_specs=(sharded, P(WIN)) + (P(),) * 11 + (sharded,),
        out_specs=(sharded, sharded) + (P(),) * 11,
        check_vma=False,
    )
```

```python
import functools
import math

import jax
import jax.numpy as jnp
import numpy as np
from jax import lax
from jax.experimental import pallas as pl
from jax.experimental.pallas import tpu as pltpu
from jax.sharding import Mesh
from jax.sharding import PartitionSpec as P

HEADS = 16
HEAD_DIM = 32
HALF = HEAD_DIM // 2
PARTS = 3 * HEAD_DIM
LENGTH = 2048
epsilon = 1e-05
masked_score = -1e30
BF = jnp.bfloat16
F32 = jnp.float32
inv_root = HEAD_DIM ** (-0.5)
score_scale = inv_root * math.log2(math.e)
VMEM_LIMIT = 60 * 1024 * 1024


def cost(flops, nbytes=1 << 20):
    return pl.CostEstimate(flops=flops, bytes_accessed=nbytes, transcendentals=0)


def mm(a, b):
    return jnp.dot(a, b, preferred_element_type=F32)


def mm_nt(a, b):
    return lax.dot_general(a, b, (((1,), (1,)), ((), ())), preferred_element_type=F32)


def mm_tn(a, b):
    return lax.dot_general(a, b, (((0,), (0,)), ((), ())), preferred_element_type=F32)


def normalize(x):
    center = x - jnp.mean(x, -1, keepdims=True)
    rstd = lax.rsqrt(jnp.mean(center * center, -1, keepdims=True) + epsilon)
    return center * rstd, rstd


def norm_back(dh, gain, xhat, rstd):
    dxhat = dh * gain
    a = jnp.mean(dxhat, -1, keepdims=True)
    b = jnp.mean(dxhat * xhat, -1, keepdims=True)
    return rstd * (dxhat - a - xhat * b)


def rotate(block, cosine, sine):
    a, b = block[:HALF], block[HALF:]
    return jnp.concatenate([a * cosine - b * sine, b * cosine + a * sine], 0)


def head_of(number):
    return number // 8


def core_of(number):
    return number // 8 % 2


def y_of(number):
    return number // 2 % 4


def qkv_kernel(place, tok, gain, bias, wq, wk, wv, cosine, sine, out):
    xhat, _ = normalize(tok[...].astype(F32))
    h1 = (xhat * gain[...] + bias[...]).astype(BF)
    cos = jnp.concatenate([cosine[...]] * 2, 1)
    sin = jnp.concatenate([sine[...]] * 2, 1)
    for n, w in enumerate((wq, wk, wv)):
        t = mm(h1, w[...]).T
        for h in range(HEADS):
            block = t[h * HEAD_DIM : (h + 1) * HEAD_DIM]
            if n < 2:
                block = rotate(block, cos, sin)
            block = block.astype(BF)
            for k in range(2):
                out[h, k, n * HEAD_DIM : (n + 1) * HEAD_DIM, :] = block[:, k * 128 : (k + 1) * 128]


def whole(*shape):
    return pl.BlockSpec(shape, lambda *_: (0,) * len(shape))


def qkv_call(place, tok, gain, bias, wq, wk, wv, cos, sin):
    rows, width = tok.shape
    table = pl.BlockSpec((HALF, 128), lambda i, p: (0, head_of(p[0])))
    return pl.pallas_call(
        qkv_kernel,
        grid_spec=pltpu.PrefetchScalarGridSpec(
            num_scalar_prefetch=1,
            grid=(1,),
            in_specs=[whole(rows, width)]
            + [whole(1, width)] * 2
            + [whole(width, width)] * 3
            + [table, table],
            out_specs=whole(HEADS, 2, PARTS, 128),
        ),
        out_shape=jax.ShapeDtypeStruct((HEADS, 2, PARTS, 128), BF),
        cost_estimate=cost(2 * rows * width * width * 3),
        compiler_params=pltpu.CompilerParams(vmem_limit_bytes=VMEM_LIMIT),
        name="qkv_forward",
    )(place, tok, gain, bias, wq, wk, wv, cos, sin)


def gather_rows(ref, w, lo, n):
    return jnp.concatenate([ref[s, w, lo : lo + n, :] for s in range(HEADS)], axis=1)


def split2(x):
    hi = x.astype(BF)
    return hi, (x - hi.astype(F32)).astype(BF)


def split3(x):
    hi = x.astype(BF)
    rest = x - hi.astype(F32)
    mid = rest.astype(BF)
    return hi, mid, (rest - mid.astype(F32)).astype(BF)


def key_rows(kt, length):
    place = lax.broadcasted_iota(jnp.int32, (16, LENGTH), 1)
    row = lax.broadcasted_iota(jnp.int32, (16, LENGTH), 0)
    mask = jnp.where(place < length, 0.0, masked_score)
    extra = jnp.where(row == 0, mask, jnp.where(row < 4, 1.0, 0.0)).astype(BF)
    zeros = jnp.zeros((48, LENGTH), BF)
    return jnp.concatenate([kt, kt, extra, zeros], 0).T


TQ = 512
TB = 512
KB = 512


KC = 256


def attend_kernel(lengths, qkv, out, mixed, total, kaug, qaug, vaug, one, two):
    for w in range(2):
        kt = gather_rows(qkv, w, 32, 32)
        kaug[...] = key_rows(kt, lengths[w])
        qs = gather_rows(qkv, w, 0, 32).astype(F32) * score_scale
        hi, lo = split2(qs)
        row = lax.broadcasted_iota(jnp.int32, (64, LENGTH), 0)
        qaug[...] = jnp.concatenate([hi, lo, jnp.where(row == 0, 1.0, 0.0).astype(BF)], 0)
        row = lax.broadcasted_iota(jnp.int32, (16, LENGTH), 0)
        vaug[...] = jnp.concatenate(
            [gather_rows(qkv, w, 64, 32), jnp.where(row == 0, 1.0, 0.0).astype(BF)], 0
        )

        def scores(t, ref, keys):
            s = mm(kaug[keys, :], qaug[:, pl.ds(pl.multiple_of(t * TQ, TQ), TQ)])
            ref[keys, :] = s
            return jnp.max(s, 0, keepdims=True)

        def tile(t, now, later, peak):
            cols = pl.ds(pl.multiple_of(t * TQ, TQ), TQ)
            after = lax.rem(t + 1, LENGTH // TQ)
            next_peak = jnp.full((1, TQ), masked_score, F32)
            o = jnp.zeros((48, TQ), F32)
            for c in range(LENGTH // KC):
                keys = slice(c * KC, (c + 1) * KC)
                next_peak = jnp.maximum(next_peak, scores(after, later, keys))
                p = jnp.exp2(now[keys, :] - peak).astype(BF)
                o = o + mm(vaug[:, keys], p)
            norm = o[32:33]
            ot = o[:32] / norm
            mixed[w, :, cols] = ot
            total[w, :, cols] = peak + jnp.log2(norm)
            for j in range(TQ // 128):
                out[t * (TQ // 128) + j, w] = ot[:, j * 128 : (j + 1) * 128].astype(BF)
            return next_peak

        peak = scores(0, one, slice(0, LENGTH))

        def pair(k, peak):
            return tile(2 * k + 1, two, one, tile(2 * k, one, two, peak))

        lax.fori_loop(0, LENGTH // TQ // 2, pair, peak)


SMEM = pl.BlockSpec(memory_space=pltpu.SMEM)
VM = pl.BlockSpec(memory_space=pltpu.VMEM)


def attend_call(lengths, qkv):
    return pl.pallas_call(
        attend_kernel,
        out_shape=(
            jax.ShapeDtypeStruct((HEADS, 2, HEAD_DIM, 128), BF),
            jax.ShapeDtypeStruct((2, HEAD_DIM, LENGTH), F32),
            jax.ShapeDtypeStruct((2, 1, LENGTH), F32),
        ),
        in_specs=[SMEM, VM],
        out_specs=(VM, VM, VM),
        scratch_shapes=[
            pltpu.VMEM((LENGTH, 128), BF),
            pltpu.VMEM((128, LENGTH), BF),
            pltpu.VMEM((48, LENGTH), BF),
            pltpu.VMEM((LENGTH, TQ), F32),
            pltpu.VMEM((LENGTH, TQ), F32),
        ],
        cost_estimate=cost(1 << 34),
        compiler_params=pltpu.CompilerParams(vmem_limit_bytes=VMEM_LIMIT),
        name="attend_forward",
    )(lengths, qkv)


def attend_back_kernel(
    lengths, qkv, dot_in, mixed, total, cosine, sine, out, rows, kaug, vaug, keys, dkt, dvt, one, two
):
    row = lax.broadcasted_iota(jnp.int32, (16, LENGTH), 0)

    def rows_of(*values):
        block = jnp.zeros((16, LENGTH), F32)
        for n, v in enumerate(values):
            block = jnp.where(row == n, v, block)
        return block.astype(BF)

    def zeros(n):
        return jnp.zeros((n, LENGTH), BF)

    def window(w, carry):
        qt = gather_rows(qkv, w, 0, 32)
        kt = gather_rows(qkv, w, 32, 32)
        do = gather_rows(dot_in, w, 0, 32)
        hi, lo = split2(qt.astype(F32) * score_scale)
        less = [v.astype(F32) for v in split3(-total[w])]
        delta = jnp.sum(do.astype(F32) * mixed[w], 0, keepdims=True)
        off = [v.astype(F32) for v in split3(-delta)]
        rows[...] = jnp.concatenate([hi, lo, rows_of(1.0, *less), do, rows_of(*off)], 0).T
        place = lax.broadcasted_iota(jnp.int32, (16, LENGTH), 1)
        mask = jnp.where(place < lengths[w], 0.0, masked_score)
        kaug[...] = jnp.concatenate([kt, kt, rows_of(mask, 1.0, 1.0, 1.0), zeros(48)], 0)
        vaug[...] = jnp.concatenate(
            [zeros(80), gather_rows(qkv, w, 64, 32), rows_of(1.0, 1.0, 1.0)], 0
        )
        keys[...] = jnp.concatenate([kt, zeros(96)], 0).T
        dkt[...] = jnp.zeros_like(dkt)
        dvt[...] = jnp.zeros_like(dvt)

        def weights(t, ref, at):
            r = rows[t * TB : (t + 1) * TB, :]
            probs = jnp.exp2(mm(r, kaug[:, at]))
            ref[0, :, at] = (probs * mm(r, vaug[:, at])).astype(BF)
            ref[1, :, at] = probs.astype(BF)

        def tile(t, now, later):
            blocks = range(t * (TB // 128), (t + 1) * (TB // 128))
            q = jnp.concatenate([qkv[j, w, 0:32, :] for j in blocks], 1)
            do_t = jnp.concatenate([dot_in[j, w] for j in blocks], 1)
            dq = jnp.zeros((TB, 128), F32)
            for c in range(LENGTH // KB):
                at = slice(c * KB, (c + 1) * KB)
                if later is not None:
                    weights(t + 1, later, at)
                ds = now[0, :, at]
                dq = dq + mm(ds, keys[at, :])
                dkt[:, at] += mm(q, ds)
                dvt[:, at] += mm(do_t, now[1, :, at])
            cols = slice(t * TB, (t + 1) * TB)
            dq = rotate((dq * inv_root).T[:32], cosine[:, cols], -sine[:, cols])
            for j, s in enumerate(blocks):
                out[s, w, 0:32, :] = dq[:, j * 128 : (j + 1) * 128].astype(BF)

        tiles = LENGTH // TB
        for c in range(LENGTH // KB):
            weights(0, one, slice(c * KB, (c + 1) * KB))
        for t in range(tiles):
            now, later = ((one, two), (two, one))[t % 2]
            tile(t, now, later if t + 1 < tiles else None)
        dk = rotate(dkt[...] * inv_root, cosine[...], -sine[...]).astype(BF)
        dv = dvt[...].astype(BF)
        for s in range(HEADS):
            out[s, w, 32:64, :] = dk[:, s * 128 : (s + 1) * 128]
            out[s, w, 64:96, :] = dv[:, s * 128 : (s + 1) * 128]
        return carry

    lax.fori_loop(0, 2, window, 0)


def attend_back_call(lengths, qkv, do, mixed, total, cos, sin):
    return pl.pallas_call(
        attend_back_kernel,
        out_shape=jax.ShapeDtypeStruct((HEADS, 2, PARTS, 128), BF),
        in_specs=[SMEM] + [VM] * 6,
        out_specs=VM,
        scratch_shapes=[
            pltpu.VMEM((LENGTH, 128), BF),
            pltpu.VMEM((128, LENGTH), BF),
            pltpu.VMEM((128, LENGTH), BF),
            pltpu.VMEM((LENGTH, 128), BF),
            pltpu.VMEM((HEAD_DIM, LENGTH), F32),
            pltpu.VMEM((HEAD_DIM, LENGTH), F32),
            pltpu.VMEM((2, TB, LENGTH), BF),
            pltpu.VMEM((2, TB, LENGTH), BF),
        ],
        cost_estimate=cost(1 << 34),
        compiler_params=pltpu.CompilerParams(vmem_limit_bytes=VMEM_LIMIT),
        name="attend_backward",
    )(lengths, qkv, do, mixed, total, cos, sin)


def ordered(ref, core, y):
    rows = []
    for o in range(2):
        for d in range(4):
            start = (core + o) % 2 * 256 + (y + d) % 4 * 64
            rows.append(ref[pl.ds(pl.multiple_of(start, 64), 64), :])
    return jnp.concatenate(rows, 0)


def pack(refs, index, value):
    for o in range(2):
        for d in range(4):
            for j in range(4):
                for l in range(4):
                    lo = o * 256 + d * 64 + j * 16
                    refs[o * 4 + d][(4 * j + l,) + index] = value[
                        lo : lo + 16, l * 128 : (l + 1) * 128
                    ].astype(BF)


def unpack(ref, index, out, where):
    for j in range(4):
        for l in range(4):
            out[where + (slice(j * 16, j * 16 + 16), slice(l * 128, l * 128 + 128))] = ref[
                (4 * j + l,) + index
            ].astype(F32)


FC = 512


def ff_kernel(
    place, tok, ob, wout, gain, bias, wg, wu, wd, cot,
    output, k0, k1, k2, k3, s0, s1, s2, s3, gwout, vecs, dres, dot_out,
    res, h2, h2t, dh2, obt, mt,
):
    pieces = (k0, k1, k2, k3, s0, s1, s2, s3)
    core, y = core_of(place[0]), y_of(place[0])
    step = pl.program_id(0)
    last = pl.num_programs(0) - 1

    @pl.when(step == 0)
    def first():
        for k in range(2):
            obt[:, k * 128 : (k + 1) * 128] = ob[:, k].reshape(512, 128)
        r = tok[...].astype(F32) + mm(obt[...].T, wout[...])
        xhat, _ = normalize(r)
        h = (xhat * gain[...] + bias[...]).astype(BF)
        res[...] = r
        h2[...] = h
        mt[...] = h.T
        h2t[...] = ordered(mt, core, y)
        output[...] = r
        dh2[...] = jnp.zeros_like(dh2)

    gate = mm(h2[...], wg[...])
    up = mm(h2[...], wu[...])
    dm = mm_nt(cot[...], wd[...])
    sg = jax.nn.sigmoid(gate)
    act = gate * sg
    m = (act * up).astype(BF)
    dgate = (dm * up * (sg * (1.0 + gate - act))).astype(BF)
    dup = (dm * act).astype(BF)
    output[...] += mm(m, wd[...])
    mt[...] = m.T
    pack(pieces, (0, 0), mm(h2t[...], dgate))
    pack(pieces, (1, 0), mm(h2t[...], dup))
    pack(pieces, (2, 0), mm(ordered(mt, core, y), cot[...]))
    dh2[...] += mm_nt(dgate, wg[...]) + mm_nt(dup, wu[...])

    @pl.when(step == last)
    def final():
        xhat, rstd = normalize(res[...])
        dh = dh2[...]
        vecs[0:1] = jnp.sum(dh * xhat, 0, keepdims=True)
        vecs[1:2] = jnp.sum(dh, 0, keepdims=True)
        dr = cot[...].astype(F32) + norm_back(dh, gain[...], xhat, rstd)
        dres[...] = dr
        da = dr.astype(BF)
        gwout[...] = mm(ordered(obt, core, y), da)
        do = mm_nt(wout[...], da).astype(BF)
        for k in range(2):
            dot_out[:, k] = do[:, k * 128 : (k + 1) * 128].reshape(HEADS, HEAD_DIM, 128)


def ff_call(place, tok, ob, wout, gain, bias, wg, wu, wd, cot):
    rows, width = tok.shape
    ff = wg.shape[1]

    return pl.pallas_call(
        ff_kernel,
        grid_spec=pltpu.PrefetchScalarGridSpec(
            num_scalar_prefetch=1,
            grid=(ff // FC,),
            in_specs=[
                whole(rows, width),
                whole(HEADS, 2, HEAD_DIM, 128),
                whole(width, width),
                whole(1, width),
                whole(1, width),
                pl.BlockSpec((width, FC), lambda i, c: (0, i)),
                pl.BlockSpec((width, FC), lambda i, c: (0, i)),
                pl.BlockSpec((FC, width), lambda i, c: (i, 0)),
                whole(rows, width),
            ],
            out_specs=(
                whole(rows, width),
            )
            + (pl.BlockSpec((16, 3, 1, 16, 128), lambda i, c: (0, 0, i, 0, 0)),) * 8
            + (
                whole(width, width),
                whole(2, width),
                whole(rows, width),
                whole(HEADS, 2, HEAD_DIM, 128),
            ),
            scratch_shapes=[
                pltpu.VMEM((rows, width), F32),
                pltpu.VMEM((rows, width), BF),
                pltpu.VMEM((width, rows), BF),
                pltpu.VMEM((rows, width), F32),
                pltpu.VMEM((width, rows), BF),
                pltpu.VMEM((FC, rows), BF),
            ],
        ),
        out_shape=(
            jax.ShapeDtypeStruct((rows, width), F32),
        )
        + (jax.ShapeDtypeStruct((16, 3, 4, 16, 128), BF),) * 8
        + (
            jax.ShapeDtypeStruct((width, width), F32),
            jax.ShapeDtypeStruct((2, width), F32),
            jax.ShapeDtypeStruct((rows, width), F32),
            jax.ShapeDtypeStruct((HEADS, 2, HEAD_DIM, 128), BF),
        ),
        cost_estimate=cost(2 * rows * width * ff * 9),
        compiler_params=pltpu.CompilerParams(vmem_limit_bytes=VMEM_LIMIT),
        name="feed_forward",
    )(place, tok, ob, wout, gain, bias, wg, wu, wd, cot)


def proj_back_kernel(place, tok, dres, dqkv, wq, wk, wv, gain, bias, gwout, vecs, gtok, *rest):
    pieces, h1t = rest[:8], rest[8]
    xhat, rstd = normalize(tok[...].astype(F32))
    h1t[...] = (xhat * gain[...] + bias[...]).astype(BF).T
    h = ordered(h1t, core_of(place[0]), y_of(place[0]))
    total = None
    for n, w in enumerate((wq, wk, wv)):
        lo = n * HEAD_DIM
        d = jnp.concatenate(
            [dqkv[:, k, lo : lo + HEAD_DIM, :].reshape(512, 128) for k in range(2)], 1
        )
        part = mm(w[...], d)
        total = part if total is None else total + part
        pack(pieces, (n,), mm_nt(h, d))
    pack(pieces, (3,), gwout[...])
    dh = total.T
    four = jnp.concatenate(
        [jnp.sum(dh * xhat, 0, keepdims=True), jnp.sum(dh, 0, keepdims=True), vecs[...]], 0
    )
    block = jnp.concatenate([four[:, l * 128 : (l + 1) * 128] for l in range(4)], 0).astype(BF)
    for ref in pieces:
        for j in range(16):
            ref[j, 4] = block
    gtok[...] = dres[...] + norm_back(dh, gain[...], xhat, rstd)


def proj_back_call(place, tok, dres, dqkv, wq, wk, wv, gain, bias, gwout, vecs):
    rows, width = tok.shape
    piece = jax.ShapeDtypeStruct((16, 5, 16, 128), BF)
    return pl.pallas_call(
        proj_back_kernel,
        out_shape=(jax.ShapeDtypeStruct((rows, width), F32),) + (piece,) * 8,
        in_specs=[SMEM] + [VM] * 10,
        out_specs=(VM,) * 9,
        scratch_shapes=[pltpu.VMEM((width, rows), BF)],
        cost_estimate=cost(2 * rows * width * width * 6),
        compiler_params=pltpu.CompilerParams(vmem_limit_bytes=VMEM_LIMIT),
        name="projection_backward",
    )(place, tok, dres, dqkv, wq, wk, wv, gain, bias, gwout, vecs)


def unpack_ff_kernel(place, *refs):
    pieces = refs[:8]
    gwg, gwu, gwd, parts, arrived = refs[8:]
    step = pl.program_id(0)
    copies = [
        pltpu.make_async_copy(piece, parts.at[k], arrived.at[k]) for k, piece in enumerate(pieces)
    ]

    @pl.when(step == 0)
    def begin():
        for copy in copies:
            copy.start()

    for k, copy in enumerate(copies):
        pl.when(step == k)(copy.wait)
    for j in range(4):
        rows = slice(j * 16, j * 16 + 16)
        for l in range(4):
            for i in range(4):
                lo = i * 512 + l * 128
                gwg[0, rows, lo : lo + 128] = parts[step, 4 * j + l, 0, i].astype(F32)
                gwu[0, rows, lo : lo + 128] = parts[step, 4 * j + l, 1, i].astype(F32)
                gwd[i, 0, rows, l * 128 : (l + 1) * 128] = parts[step, 4 * j + l, 2, i].astype(F32)


def unpack_ff_call(place, pieces):
    def spec(block, axis):
        def index(k, p):
            at = [0] * len(block)
            at[axis] = (core_of(p[0]) + k // 4) % 2 * 4 + (y_of(p[0]) + 4 - k % 4) % 4
            return tuple(at)

        return pl.BlockSpec(block, index)

    return pl.pallas_call(
        unpack_ff_kernel,
        grid_spec=pltpu.PrefetchScalarGridSpec(
            num_scalar_prefetch=1,
            grid=(8,),
            in_specs=[pl.BlockSpec(memory_space=pl.ANY)] * 8,
            out_specs=(
                spec((1, 64, 2048), 0),
                spec((1, 64, 2048), 0),
                spec((4, 1, 64, 512), 1),
            ),
            scratch_shapes=[
                pltpu.VMEM((8,) + pieces[0].shape, BF),
                pltpu.SemaphoreType.DMA((8,)),
            ],
        ),
        out_shape=(
            jax.ShapeDtypeStruct((8, 64, 2048), F32),
            jax.ShapeDtypeStruct((8, 64, 2048), F32),
            jax.ShapeDtypeStruct((4, 8, 64, 512), F32),
        ),
        cost_estimate=cost(1 << 20, 18 << 20),
        compiler_params=pltpu.CompilerParams(vmem_limit_bytes=VMEM_LIMIT),
        name="unpack_feed_forward",
    )(place, *pieces)


def unpack_kernel(place, *refs):
    outs = refs[-4:]
    core, y = core_of(place[0]), y_of(place[0])
    for d in range(4):
        start = (y + 4 - d) % 4 * 64
        for ref, c in ((refs[d], core), (refs[4 + d], 1 - core)):
            for n, g in enumerate(outs):
                for j in range(4):
                    rows = pl.ds(pl.multiple_of(c * 256 + start + j * 16, 16), 16)
                    for l in range(4):
                        g[rows, l * 128 : (l + 1) * 128] = ref[4 * j + l, n].astype(F32)


def unpack_call(place, mine, others):
    square = jax.ShapeDtypeStruct((512, 512), F32)
    return pl.pallas_call(
        unpack_kernel,
        out_shape=(square,) * 4,
        in_specs=[SMEM] + [VM] * 8,
        out_specs=(VM,) * 4,
        cost_estimate=cost(1 << 20, 6 << 20),
        compiler_params=pltpu.CompilerParams(vmem_limit_bytes=VMEM_LIMIT),
        name="unpack_projections",
    )(place, *mine, *others)


def angles():
    inverse = np.float32(10000.0) ** (-np.arange(HALF, dtype=np.float32) * np.float32(2.0 / HEAD_DIM))
    turn = inverse[:, None] * np.arange(LENGTH, dtype=np.float32)[None, :]
    turn = turn.astype(np.float64)
    return np.cos(turn).astype(np.float32), np.sin(turn).astype(np.float32)


SEQ = ("x", "zh", "c")
WIN = ("y", "zl")
REST = ("zl", "zh", "x")
SWAP = [(0, 1), (1, 0)]


def exchange(x, axes):
    return lax.all_to_all(x, axes, 0, 0, tiled=True)


def spread(x, axes, n):
    return exchange(jnp.broadcast_to(x[None], (n,) + x.shape), axes)


def add_up(*terms):
    return sum(t.astype(F32) for t in terms).astype(BF)


def along_y(x, d):
    return lax.ppermute(x, "y", [(i, (i + d) % 4) for i in range(4)])


def reduce_y(pieces):
    got = [lax.ppermute(p, "c", SWAP) for p in pieces[4:]]
    there = [along_y(add_up(pieces[d], got[d]), d) for d in (1, 2, 3)]
    return add_up(pieces[0], got[0], *there)


def reduce_rest(x):
    return jnp.sum(exchange(x, REST).astype(F32), 0).astype(BF)


def collect(whole_piece):
    mine = [whole_piece] + [along_y(whole_piece, d) for d in (1, 2, 3)]
    return mine, [lax.ppermute(m, "c", SWAP) for m in mine]


def after(x, *others):
    return lax.optimization_barrier((x,) + others)[0]


def local(
    tokens, lengths, gain_one, bias_one, weight_query, weight_key, weight_value, weight_out,
    gain_two, bias_two, weight_gate, weight_up, weight_down, cotangent,
):
    win_count, seq_rows, width = tokens.shape
    rows = win_count * seq_rows
    tok = tokens.reshape(rows, width)
    cot = cotangent.reshape(rows, width)
    g1, b1, g2, b2 = (v.reshape(1, width) for v in (gain_one, bias_one, gain_two, bias_two))
    cos, sin = angles()
    place = lax.axis_index(SEQ + WIN).reshape(1)

    sent = qkv_call(place, tok, g1, b1, weight_query, weight_key, weight_value, cos, sin)
    qkv = exchange(sent, SEQ)
    mixed_low, mixed, total = attend_call(lengths, qkv)
    ob = exchange(mixed_low, SEQ)
    output, *pieces, gwout, vecs, dres, dot_out = ff_call(
        place, tok, ob, weight_out, g2, b2, weight_gate, weight_up, weight_down, cot
    )
    do = exchange(dot_out, SEQ)
    ff = reduce_y(pieces)
    dqkv = exchange(attend_back_call(lengths, qkv, do, mixed, total, cos, sin), SEQ)
    ff = reduce_rest(after(ff, dqkv))
    gtok, *pieces = proj_back_call(
        place, tok, dres, dqkv, weight_query, weight_key, weight_value, g1, b1, gwout, vecs
    )
    ff = spread(ff, REST, 16)
    mine, others = collect(ff)
    gwg, gwu, gwd = unpack_ff_call(place, mine + others)
    part = reduce_rest(after(reduce_y(pieces), ff))
    four = part[4].reshape(4, 4, 128).transpose(1, 0, 2).reshape(4, width).astype(F32)
    gwq, gwk, gwv, gwout = unpack_call(place, *collect(spread(part[:4], REST, 16)))
    return (
        output.reshape(tokens.shape),
        gtok.reshape(tokens.shape),
        four[0],
        four[1],
        gwq,
        gwk,
        gwv,
        gwout,
        four[2],
        four[3],
        gwg.reshape(width, 2048),
        gwu.reshape(width, 2048),
        gwd.reshape(2048, width),
    )


def solution(mesh):
    fine = Mesh(mesh.devices.reshape(4, 2, 2, 4, 2), SEQ + WIN)
    sharded = P(WIN, SEQ, None)
    return jax.shard_map(
        local,
        mesh=fine,
        in_specs=(sharded, P(WIN)) + (P(),) * 11 + (sharded,),
        out_specs=(sharded, sharded) + (P(),) * 11,
        check_vma=False,
    )
```

```python
import functools
import math

import jax
import jax.numpy as jnp
import numpy as np
from jax import lax
from jax.experimental import pallas as pl
from jax.experimental.pallas import tpu as pltpu
from jax.sharding import Mesh
from jax.sharding import PartitionSpec as P

HEADS = 16
HEAD_DIM = 32
HALF = HEAD_DIM // 2
PARTS = 3 * HEAD_DIM
LENGTH = 2048
epsilon = 1e-05
masked_score = -1e30
BF = jnp.bfloat16
F32 = jnp.float32
inv_root = HEAD_DIM ** (-0.5)
score_scale = inv_root * math.log2(math.e)
VMEM_LIMIT = 60 * 1024 * 1024


def cost(flops, nbytes=1 << 20):
    return pl.CostEstimate(flops=flops, bytes_accessed=nbytes, transcendentals=0)


def mm(a, b):
    return jnp.dot(a, b, preferred_element_type=F32)


def mm_nt(a, b):
    return lax.dot_general(a, b, (((1,), (1,)), ((), ())), preferred_element_type=F32)


def mm_tn(a, b):
    return lax.dot_general(a, b, (((0,), (0,)), ((), ())), preferred_element_type=F32)


def normalize(x):
    center = x - jnp.mean(x, -1, keepdims=True)
    rstd = lax.rsqrt(jnp.mean(center * center, -1, keepdims=True) + epsilon)
    return center * rstd, rstd


def norm_back(dh, gain, xhat, rstd):
    dxhat = dh * gain
    a = jnp.mean(dxhat, -1, keepdims=True)
    b = jnp.mean(dxhat * xhat, -1, keepdims=True)
    return rstd * (dxhat - a - xhat * b)


def rotate(block, cosine, sine):
    a, b = block[:HALF], block[HALF:]
    return jnp.concatenate([a * cosine - b * sine, b * cosine + a * sine], 0)


def head_of(number):
    return number // 8


def core_of(number):
    return number // 8 % 2


def y_of(number):
    return number // 2 % 4


def qkv_kernel(place, tok, gain, bias, wq, wk, wv, cosine, sine, out):
    xhat, _ = normalize(tok[...].astype(F32))
    h1 = (xhat * gain[...] + bias[...]).astype(BF)
    cos = jnp.concatenate([cosine[...]] * 2, 1)
    sin = jnp.concatenate([sine[...]] * 2, 1)
    for n, w in enumerate((wq, wk, wv)):
        t = mm(h1, w[...]).T
        for h in range(HEADS):
            block = t[h * HEAD_DIM : (h + 1) * HEAD_DIM]
            if n < 2:
                block = rotate(block, cos, sin)
            block = block.astype(BF)
            for k in range(2):
                out[h, k, n * HEAD_DIM : (n + 1) * HEAD_DIM, :] = block[:, k * 128 : (k + 1) * 128]


def whole(*shape):
    return pl.BlockSpec(shape, lambda *_: (0,) * len(shape))


def qkv_call(place, tok, gain, bias, wq, wk, wv, cos, sin):
    rows, width = tok.shape
    table = pl.BlockSpec((HALF, 128), lambda i, p: (0, head_of(p[0])))
    return pl.pallas_call(
        qkv_kernel,
        grid_spec=pltpu.PrefetchScalarGridSpec(
            num_scalar_prefetch=1,
            grid=(1,),
            in_specs=[whole(rows, width)]
            + [whole(1, width)] * 2
            + [whole(width, width)] * 3
            + [table, table],
            out_specs=whole(HEADS, 2, PARTS, 128),
        ),
        out_shape=jax.ShapeDtypeStruct((HEADS, 2, PARTS, 128), BF),
        cost_estimate=cost(2 * rows * width * width * 3),
        compiler_params=pltpu.CompilerParams(vmem_limit_bytes=VMEM_LIMIT),
        name="qkv_forward",
    )(place, tok, gain, bias, wq, wk, wv, cos, sin)


def gather_rows(ref, w, lo, n):
    return jnp.concatenate([ref[s, w, lo : lo + n, :] for s in range(HEADS)], axis=1)


def split2(x):
    hi = x.astype(BF)
    return hi, (x - hi.astype(F32)).astype(BF)


def split3(x):
    hi = x.astype(BF)
    rest = x - hi.astype(F32)
    mid = rest.astype(BF)
    return hi, mid, (rest - mid.astype(F32)).astype(BF)


def key_rows(kt, length):
    place = lax.broadcasted_iota(jnp.int32, (16, LENGTH), 1)
    row = lax.broadcasted_iota(jnp.int32, (16, LENGTH), 0)
    mask = jnp.where(place < length, 0.0, masked_score)
    extra = jnp.where(row == 0, mask, jnp.where(row < 4, 1.0, 0.0)).astype(BF)
    zeros = jnp.zeros((48, LENGTH), BF)
    return jnp.concatenate([kt, kt, extra, zeros], 0).T


TQ = 512
TB = 512
KB = 512


KC = 256


def attend_kernel(lengths, qkv, out, mixed, total, kaug, qaug, vaug, one, two):
    for w in range(2):
        kt = gather_rows(qkv, w, 32, 32)
        kaug[...] = key_rows(kt, lengths[w])
        qs = gather_rows(qkv, w, 0, 32).astype(F32) * score_scale
        hi, lo = split2(qs)
        row = lax.broadcasted_iota(jnp.int32, (64, LENGTH), 0)
        qaug[...] = jnp.concatenate([hi, lo, jnp.where(row == 0, 1.0, 0.0).astype(BF)], 0)
        row = lax.broadcasted_iota(jnp.int32, (16, LENGTH), 0)
        vaug[...] = jnp.concatenate(
            [gather_rows(qkv, w, 64, 32), jnp.where(row == 0, 1.0, 0.0).astype(BF)], 0
        )

        def scores(t, ref, keys):
            s = mm(kaug[keys, :], qaug[:, pl.ds(pl.multiple_of(t * TQ, TQ), TQ)])
            ref[keys, :] = s
            return jnp.max(s, 0, keepdims=True)

        def tile(t, now, later, peak):
            cols = pl.ds(pl.multiple_of(t * TQ, TQ), TQ)
            after = lax.rem(t + 1, LENGTH // TQ)
            next_peak = jnp.full((1, TQ), masked_score, F32)
            o = jnp.zeros((48, TQ), F32)
            for c in range(LENGTH // KC):
                keys = slice(c * KC, (c + 1) * KC)
                next_peak = jnp.maximum(next_peak, scores(after, later, keys))
                p = jnp.exp2(now[keys, :] - peak).astype(BF)
                o = o + mm(vaug[:, keys], p)
            norm = o[32:33]
            ot = o[:32] / norm
            mixed[w, :, cols] = ot
            total[w, :, cols] = peak + jnp.log2(norm)
            for j in range(TQ // 128):
                out[t * (TQ // 128) + j, w] = ot[:, j * 128 : (j + 1) * 128].astype(BF)
            return next_peak

        peak = scores(0, one, slice(0, LENGTH))

        def pair(k, peak):
            return tile(2 * k + 1, two, one, tile(2 * k, one, two, peak))

        lax.fori_loop(0, LENGTH // TQ // 2, pair, peak)


SMEM = pl.BlockSpec(memory_space=pltpu.SMEM)
VM = pl.BlockSpec(memory_space=pltpu.VMEM)


def attend_call(lengths, qkv):
    return pl.pallas_call(
        attend_kernel,
        out_shape=(
            jax.ShapeDtypeStruct((HEADS, 2, HEAD_DIM, 128), BF),
            jax.ShapeDtypeStruct((2, HEAD_DIM, LENGTH), F32),
            jax.ShapeDtypeStruct((2, 1, LENGTH), F32),
        ),
        in_specs=[SMEM, VM],
        out_specs=(VM, VM, VM),
        scratch_shapes=[
            pltpu.VMEM((LENGTH, 128), BF),
            pltpu.VMEM((128, LENGTH), BF),
            pltpu.VMEM((48, LENGTH), BF),
            pltpu.VMEM((LENGTH, TQ), F32),
            pltpu.VMEM((LENGTH, TQ), F32),
        ],
        cost_estimate=cost(1 << 34),
        compiler_params=pltpu.CompilerParams(vmem_limit_bytes=VMEM_LIMIT),
        name="attend_forward",
    )(lengths, qkv)


def attend_back_kernel(
    lengths, qkv, dot_in, mixed, total, cosine, sine, out, rows, kaug, vaug, keys, dkt, dvt, one, two
):
    row = lax.broadcasted_iota(jnp.int32, (16, LENGTH), 0)

    def rows_of(*values):
        block = jnp.zeros((16, LENGTH), F32)
        for n, v in enumerate(values):
            block = jnp.where(row == n, v, block)
        return block.astype(BF)

    def zeros(n):
        return jnp.zeros((n, LENGTH), BF)

    def window(w, carry):
        qt = gather_rows(qkv, w, 0, 32)
        kt = gather_rows(qkv, w, 32, 32)
        do = gather_rows(dot_in, w, 0, 32)
        hi, lo = split2(qt.astype(F32) * score_scale)
        less = [v.astype(F32) for v in split3(-total[w])]
        delta = jnp.sum(do.astype(F32) * mixed[w], 0, keepdims=True)
        off = [v.astype(F32) for v in split3(-delta)]
        rows[...] = jnp.concatenate([hi, lo, rows_of(1.0, *less), do, rows_of(*off)], 0).T
        place = lax.broadcasted_iota(jnp.int32, (16, LENGTH), 1)
        mask = jnp.where(place < lengths[w], 0.0, masked_score)
        kaug[...] = jnp.concatenate([kt, kt, rows_of(mask, 1.0, 1.0, 1.0), zeros(48)], 0)
        vaug[...] = jnp.concatenate(
            [zeros(80), gather_rows(qkv, w, 64, 32), rows_of(1.0, 1.0, 1.0)], 0
        )
        keys[...] = jnp.concatenate([kt, zeros(96)], 0).T
        dkt[...] = jnp.zeros_like(dkt)
        dvt[...] = jnp.zeros_like(dvt)

        def weights(t, ref, at):
            r = rows[t * TB : (t + 1) * TB, :]
            probs = jnp.exp2(mm(r, kaug[:, at]))
            ref[0, :, at] = (probs * mm(r, vaug[:, at])).astype(BF)
            ref[1, :, at] = probs.astype(BF)

        def tile(t, now, later):
            blocks = range(t * (TB // 128), (t + 1) * (TB // 128))
            q = jnp.concatenate([qkv[j, w, 0:32, :] for j in blocks], 1)
            do_t = jnp.concatenate([dot_in[j, w] for j in blocks], 1)
            dq = jnp.zeros((TB, 128), F32)
            for c in range(LENGTH // KB):
                at = slice(c * KB, (c + 1) * KB)
                if later is not None:
                    weights(t + 1, later, at)
                ds = now[0, :, at]
                dq = dq + mm(ds, keys[at, :])
                dkt[:, at] += mm(q, ds)
                dvt[:, at] += mm(do_t, now[1, :, at])
            cols = slice(t * TB, (t + 1) * TB)
            dq = rotate((dq * inv_root).T[:32], cosine[:, cols], -sine[:, cols])
            for j, s in enumerate(blocks):
                out[s, w, 0:32, :] = dq[:, j * 128 : (j + 1) * 128].astype(BF)

        tiles = LENGTH // TB
        for c in range(LENGTH // KB):
            weights(0, one, slice(c * KB, (c + 1) * KB))
        for t in range(tiles):
            now, later = ((one, two), (two, one))[t % 2]
            tile(t, now, later if t + 1 < tiles else None)
        dk = rotate(dkt[...] * inv_root, cosine[...], -sine[...]).astype(BF)
        dv = dvt[...].astype(BF)
        for s in range(HEADS):
            out[s, w, 32:64, :] = dk[:, s * 128 : (s + 1) * 128]
            out[s, w, 64:96, :] = dv[:, s * 128 : (s + 1) * 128]
        return carry

    lax.fori_loop(0, 2, window, 0)


def attend_back_call(lengths, qkv, do, mixed, total, cos, sin):
    return pl.pallas_call(
        attend_back_kernel,
        out_shape=jax.ShapeDtypeStruct((HEADS, 2, PARTS, 128), BF),
        in_specs=[SMEM] + [VM] * 6,
        out_specs=VM,
        scratch_shapes=[
            pltpu.VMEM((LENGTH, 128), BF),
            pltpu.VMEM((128, LENGTH), BF),
            pltpu.VMEM((128, LENGTH), BF),
            pltpu.VMEM((LENGTH, 128), BF),
            pltpu.VMEM((HEAD_DIM, LENGTH), F32),
            pltpu.VMEM((HEAD_DIM, LENGTH), F32),
            pltpu.VMEM((2, TB, LENGTH), BF),
            pltpu.VMEM((2, TB, LENGTH), BF),
        ],
        cost_estimate=cost(1 << 34),
        compiler_params=pltpu.CompilerParams(vmem_limit_bytes=VMEM_LIMIT),
        name="attend_backward",
    )(lengths, qkv, do, mixed, total, cos, sin)


def ordered(ref, core, y):
    rows = []
    for o in range(2):
        for d in range(4):
            start = (core + o) % 2 * 256 + (y + d) % 4 * 64
            rows.append(ref[pl.ds(pl.multiple_of(start, 64), 64), :])
    return jnp.concatenate(rows, 0)


def pack(refs, index, value):
    for o in range(2):
        for d in range(4):
            for j in range(4):
                for l in range(4):
                    lo = o * 256 + d * 64 + j * 16
                    refs[o * 4 + d][(4 * j + l,) + index] = value[
                        lo : lo + 16, l * 128 : (l + 1) * 128
                    ].astype(BF)


def unpack(ref, index, out, where):
    for j in range(4):
        for l in range(4):
            out[where + (slice(j * 16, j * 16 + 16), slice(l * 128, l * 128 + 128))] = ref[
                (4 * j + l,) + index
            ].astype(F32)


FC = 512


def ff_kernel(
    place, tok, ob, wout, gain, bias, wg_all, wu_all, wd_all, cot,
    output, k0, k1, k2, k3, s0, s1, s2, s3, gwout, vecs, dres, dot_out,
    h2t, dh2, obt, mt, wg_here, wu_here, wd_here, arrived,
):
    pieces = (k0, k1, k2, k3, s0, s1, s2, s3)
    core, y = core_of(place[0]), y_of(place[0])
    steps = wg_all.shape[1] // FC

    def copies(i):
        at = slice(i * FC, (i + 1) * FC)
        return (
            pltpu.make_async_copy(wg_all.at[:, at], wg_here.at[i], arrived.at[3 * i]),
            pltpu.make_async_copy(wu_all.at[:, at], wu_here.at[i], arrived.at[3 * i + 1]),
            pltpu.make_async_copy(wd_all.at[at, :], wd_here.at[i], arrived.at[3 * i + 2]),
        )

    for i in range(steps):
        for copy in copies(i):
            copy.start()
    for k in range(2):
        obt[:, k * 128 : (k + 1) * 128] = ob[:, k].reshape(512, 128)
    r = tok[...].astype(F32) + mm(obt[...].T, wout[...])
    xhat, rstd = normalize(r)
    h2 = (xhat * gain[...] + bias[...]).astype(BF)
    mt[...] = h2.T
    h2t[...] = ordered(mt, core, y)
    output[...] = r
    for i in range(steps):
        for copy in copies(i):
            copy.wait()
        wg, wu, wd = wg_here[i], wu_here[i], wd_here[i]
        gate = mm(h2, wg)
        up = mm(h2, wu)
        dm = mm_nt(cot[...], wd)
        sg = jax.nn.sigmoid(gate)
        act = gate * sg
        m = (act * up).astype(BF)
        dgate = (dm * up * (sg * (1.0 + gate - act))).astype(BF)
        dup = (dm * act).astype(BF)
        output[...] += mm(m, wd)
        mt[...] = m.T
        pack(pieces, (0, i), mm(h2t[...], dgate))
        pack(pieces, (1, i), mm(h2t[...], dup))
        pack(pieces, (2, i), mm(ordered(mt, core, y), cot[...]))
        part = mm_nt(dgate, wg) + mm_nt(dup, wu)
        if i == 0:
            dh2[...] = part
        else:
            dh2[...] += part
    xhat, rstd = normalize(r)
    dh = dh2[...]
    vecs[0:1] = jnp.sum(dh * xhat, 0, keepdims=True)
    vecs[1:2] = jnp.sum(dh, 0, keepdims=True)
    dr = cot[...].astype(F32) + norm_back(dh, gain[...], xhat, rstd)
    dres[...] = dr
    da = dr.astype(BF)
    gwout[...] = mm(ordered(obt, core, y), da).astype(BF)
    do = mm_nt(wout[...], da).astype(BF)
    for k in range(2):
        dot_out[:, k] = do[:, k * 128 : (k + 1) * 128].reshape(HEADS, HEAD_DIM, 128)


def ff_call(place, tok, ob, wout, gain, bias, wg, wu, wd, cot):
    rows, width = tok.shape
    ff = wg.shape[1]
    steps = ff // FC
    anywhere = pl.BlockSpec(memory_space=pl.ANY)
    return pl.pallas_call(
        ff_kernel,
        in_specs=[SMEM] + [VM] * 5 + [anywhere] * 3 + [VM],
        out_specs=(VM,) * 13,
        out_shape=(jax.ShapeDtypeStruct((rows, width), F32),)
        + (jax.ShapeDtypeStruct((16, 3, 4, 16, 128), BF),) * 8
        + (
            jax.ShapeDtypeStruct((width, width), BF),
            jax.ShapeDtypeStruct((2, width), F32),
            jax.ShapeDtypeStruct((rows, width), F32),
            jax.ShapeDtypeStruct((HEADS, 2, HEAD_DIM, 128), BF),
        ),
        scratch_shapes=[
            pltpu.VMEM((width, rows), BF),
            pltpu.VMEM((rows, width), F32),
            pltpu.VMEM((width, rows), BF),
            pltpu.VMEM((FC, rows), BF),
            pltpu.VMEM((steps, width, FC), BF),
            pltpu.VMEM((steps, width, FC), BF),
            pltpu.VMEM((steps, FC, width), BF),
            pltpu.SemaphoreType.DMA((3 * steps,)),
        ],
        cost_estimate=cost(2 * rows * width * ff * 9),
        compiler_params=pltpu.CompilerParams(vmem_limit_bytes=VMEM_LIMIT),
        name="feed_forward",
    )(place, tok, ob, wout, gain, bias, wg, wu, wd, cot)


def proj_back_kernel(place, tok, dres, dqkv, wq, wk, wv, gain, bias, gwout, vecs, gtok, *rest):
    pieces, h1t = rest[:8], rest[8]
    xhat, rstd = normalize(tok[...].astype(F32))
    h1t[...] = (xhat * gain[...] + bias[...]).astype(BF).T
    h = ordered(h1t, core_of(place[0]), y_of(place[0]))
    total = None
    for n, w in enumerate((wq, wk, wv)):
        lo = n * HEAD_DIM
        d = jnp.concatenate(
            [dqkv[:, k, lo : lo + HEAD_DIM, :].reshape(512, 128) for k in range(2)], 1
        )
        part = mm(w[...], d)
        total = part if total is None else total + part
        pack(pieces, (n,), mm_nt(h, d))
    pack(pieces, (3,), gwout[...])
    dh = total.T
    four = jnp.concatenate(
        [jnp.sum(dh * xhat, 0, keepdims=True), jnp.sum(dh, 0, keepdims=True), vecs[...]], 0
    )
    block = jnp.concatenate([four[:, l * 128 : (l + 1) * 128] for l in range(4)], 0).astype(BF)
    for ref in pieces:
        for j in range(16):
            ref[j, 4] = block
    gtok[...] = dres[...] + norm_back(dh, gain[...], xhat, rstd)


def proj_back_call(place, tok, dres, dqkv, wq, wk, wv, gain, bias, gwout, vecs):
    rows, width = tok.shape
    piece = jax.ShapeDtypeStruct((16, 5, 16, 128), BF)
    return pl.pallas_call(
        proj_back_kernel,
        out_shape=(jax.ShapeDtypeStruct((rows, width), F32),) + (piece,) * 8,
        in_specs=[SMEM] + [VM] * 10,
        out_specs=(VM,) * 9,
        scratch_shapes=[pltpu.VMEM((width, rows), BF)],
        cost_estimate=cost(2 * rows * width * width * 6),
        compiler_params=pltpu.CompilerParams(vmem_limit_bytes=VMEM_LIMIT),
        name="projection_backward",
    )(place, tok, dres, dqkv, wq, wk, wv, gain, bias, gwout, vecs)


def unpack_ff_kernel(place, *refs):
    pieces = refs[:8]
    gwg, gwu, gwd, parts, arrived = refs[8:]
    step = pl.program_id(0)
    copies = [
        pltpu.make_async_copy(piece, parts.at[k], arrived.at[k]) for k, piece in enumerate(pieces)
    ]

    @pl.when(step == 0)
    def begin():
        for copy in copies:
            copy.start()

    for k, copy in enumerate(copies):
        pl.when(step == k)(copy.wait)
    for j in range(4):
        rows = slice(j * 16, j * 16 + 16)
        for l in range(4):
            for i in range(4):
                lo = i * 512 + l * 128
                gwg[0, rows, lo : lo + 128] = parts[step, 4 * j + l, 0, i].astype(F32)
                gwu[0, rows, lo : lo + 128] = parts[step, 4 * j + l, 1, i].astype(F32)
                gwd[i, 0, rows, l * 128 : (l + 1) * 128] = parts[step, 4 * j + l, 2, i].astype(F32)


def unpack_ff_call(place, pieces):
    def spec(block, axis):
        def index(k, p):
            at = [0] * len(block)
            at[axis] = (core_of(p[0]) + k // 4) % 2 * 4 + (y_of(p[0]) + 4 - k % 4) % 4
            return tuple(at)

        return pl.BlockSpec(block, index)

    return pl.pallas_call(
        unpack_ff_kernel,
        grid_spec=pltpu.PrefetchScalarGridSpec(
            num_scalar_prefetch=1,
            grid=(8,),
            in_specs=[pl.BlockSpec(memory_space=pl.ANY)] * 8,
            out_specs=(
                spec((1, 64, 2048), 0),
                spec((1, 64, 2048), 0),
                spec((4, 1, 64, 512), 1),
            ),
            scratch_shapes=[
                pltpu.VMEM((8,) + pieces[0].shape, BF),
                pltpu.SemaphoreType.DMA((8,)),
            ],
        ),
        out_shape=(
            jax.ShapeDtypeStruct((8, 64, 2048), F32),
            jax.ShapeDtypeStruct((8, 64, 2048), F32),
            jax.ShapeDtypeStruct((4, 8, 64, 512), F32),
        ),
        cost_estimate=cost(1 << 20, 18 << 20),
        compiler_params=pltpu.CompilerParams(vmem_limit_bytes=VMEM_LIMIT),
        name="unpack_feed_forward",
    )(place, *pieces)


def unpack_kernel(place, *refs):
    outs = refs[-4:]
    core, y = core_of(place[0]), y_of(place[0])
    for d in range(4):
        start = (y + 4 - d) % 4 * 64
        for ref, c in ((refs[d], core), (refs[4 + d], 1 - core)):
            for n, g in enumerate(outs):
                for j in range(4):
                    rows = pl.ds(pl.multiple_of(c * 256 + start + j * 16, 16), 16)
                    for l in range(4):
                        g[rows, l * 128 : (l + 1) * 128] = ref[4 * j + l, n].astype(F32)


def unpack_call(place, mine, others):
    square = jax.ShapeDtypeStruct((512, 512), F32)
    return pl.pallas_call(
        unpack_kernel,
        out_shape=(square,) * 4,
        in_specs=[SMEM] + [VM] * 8,
        out_specs=(VM,) * 4,
        cost_estimate=cost(1 << 20, 6 << 20),
        compiler_params=pltpu.CompilerParams(vmem_limit_bytes=VMEM_LIMIT),
        name="unpack_projections",
    )(place, *mine, *others)


def angles():
    inverse = np.float32(10000.0) ** (-np.arange(HALF, dtype=np.float32) * np.float32(2.0 / HEAD_DIM))
    turn = inverse[:, None] * np.arange(LENGTH, dtype=np.float32)[None, :]
    turn = turn.astype(np.float64)
    return np.cos(turn).astype(np.float32), np.sin(turn).astype(np.float32)


SEQ = ("x", "zh", "c")
WIN = ("y", "zl")
REST = ("zl", "zh", "x")
SWAP = [(0, 1), (1, 0)]


def exchange(x, axes):
    return lax.all_to_all(x, axes, 0, 0, tiled=True)


def spread(x, axes, n):
    return exchange(jnp.broadcast_to(x[None], (n,) + x.shape), axes)


def add_up(*terms):
    return sum(t.astype(F32) for t in terms).astype(BF)


def along_y(x, d):
    return lax.ppermute(x, "y", [(i, (i + d) % 4) for i in range(4)])


def reduce_y(pieces):
    got = [lax.ppermute(p, "c", SWAP) for p in pieces[4:]]
    there = [along_y(add_up(pieces[d], got[d]), d) for d in (1, 2, 3)]
    return add_up(pieces[0], got[0], *there)


def reduce_rest(x):
    return jnp.sum(exchange(x, REST).astype(F32), 0).astype(BF)


def collect(whole_piece):
    mine = [whole_piece] + [along_y(whole_piece, d) for d in (1, 2, 3)]
    theirs = [lax.ppermute(m, "c", SWAP) for m in mine[::-1]]
    return mine, theirs[::-1]


def after(x, *others):
    return lax.optimization_barrier((x,) + others)[0]


def local(
    tokens, lengths, gain_one, bias_one, weight_query, weight_key, weight_value, weight_out,
    gain_two, bias_two, weight_gate, weight_up, weight_down, cotangent,
):
    win_count, seq_rows, width = tokens.shape
    rows = win_count * seq_rows
    tok = tokens.reshape(rows, width)
    cot = cotangent.reshape(rows, width)
    g1, b1, g2, b2 = (v.reshape(1, width) for v in (gain_one, bias_one, gain_two, bias_two))
    cos, sin = angles()
    place = lax.axis_index(SEQ + WIN).reshape(1)

    sent = qkv_call(place, tok, g1, b1, weight_query, weight_key, weight_value, cos, sin)
    qkv = exchange(sent, SEQ)
    mixed_low, mixed, total = attend_call(lengths, qkv)
    ob = exchange(mixed_low, SEQ)
    output, *pieces, gwout, vecs, dres, dot_out = ff_call(
        place, tok, ob, weight_out, g2, b2, weight_gate, weight_up, weight_down, cot
    )
    do = exchange(dot_out, SEQ)
    ff = reduce_y(pieces)
    dqkv = exchange(attend_back_call(lengths, qkv, do, mixed, total, cos, sin), SEQ)
    ff = reduce_rest(after(ff, dqkv))
    gtok, *pieces = proj_back_call(
        place, tok, dres, dqkv, weight_query, weight_key, weight_value, g1, b1, gwout, vecs
    )
    ff = spread(ff, REST, 16)
    mine, others = collect(ff)
    gwg, gwu, gwd = unpack_ff_call(place, mine + others)
    part = reduce_rest(after(reduce_y(pieces), ff))
    four = part[4].reshape(4, 4, 128).transpose(1, 0, 2).reshape(4, width).astype(F32)
    gwq, gwk, gwv, gwout = unpack_call(place, *collect(spread(part[:4], REST, 16)))
    return (
        output.reshape(tokens.shape),
        gtok.reshape(tokens.shape),
        four[0],
        four[1],
        gwq,
        gwk,
        gwv,
        gwout,
        four[2],
        four[3],
        gwg.reshape(width, 2048),
        gwu.reshape(width, 2048),
        gwd.reshape(2048, width),
    )


def solution(mesh):
    fine = Mesh(mesh.devices.reshape(4, 2, 2, 4, 2), SEQ + WIN)
    sharded = P(WIN, SEQ, None)
    return jax.shard_map(
        local,
        mesh=fine,
        in_specs=(sharded, P(WIN)) + (P(),) * 11 + (sharded,),
        out_specs=(sharded, sharded) + (P(),) * 11,
        check_vma=False,
    )
```
